256 devices in a mesh: dp: 32 (over x, y, core), expert: 8 (over z).
Axes of the slice: x: 4, y: 4, z: 8, core: 2. Of those that a mesh axis runs over, the one named last changes fastest.
Arguments:
- grad: bfloat16 [8, 32, 256, 8192], P('expert', 'dp'), may hold values from -23 to 23, as said below
- error: bfloat16 [8, 32, 256, 8192], P('expert', 'dp'), may hold values from -3 to 3
- q_init: bfloat16 [8, 32, 8192], P('expert'), may hold values from -4 to 4
Outputs:
- basis_out: float32 [8, 256, 32], P('expert')
- q_factor: float32 [8, 32, 8192], P('expert', None, 'dp')
- new_error: bfloat16 [8, 32, 256, 8192], P('expert', 'dp')
- error_norm: float32 [], replicated
The draws below stay inside these ranges and needn't reach their ends.
Inputs may be any that keep to these rules, and one draw needn't show every extreme that they name: `grad`: entries of each expert's gradient.
All inputs are finite; a program needn't handle non-finite values.
Results may differ from the reference program's by a relative error of at most 0.02.
Values may be sent and summed in bfloat16 or wider, within the bound.
No kernel may reach another device: no remote copies, remote signals or barrier semaphores. Data moves between devices by JAX's collectives and lax.ppermute only.
A program may use at most 64 MiB of HBM per device.

```python
import math
import jax
import jax.numpy as jnp
from jax import lax

ROWS = 256
FF = 8192
R = 32
ITERS = 2
EXPERTS = 8
REPLICAS = 32


def draw_grad(key, part):
    key = jax.random.fold_in(key, 7)
    key_base = jax.random.fold_in(key, 0)
    key_columns = jax.random.fold_in(key, 2)
    shape = (EXPERTS, REPLICAS, ROWS, FF)
    replica_ramp = jnp.arange(REPLICAS, dtype=jnp.float32) / max(REPLICAS - 1, 1)
    base = jax.random.truncated_normal(key_base, -4.0, 4.0, shape, jnp.float32)
    replica_scale = 0.5 * jnp.exp(replica_ramp * math.log(4.0))
    columns = jnp.exp(jax.random.uniform(key_columns, (EXPERTS, 1, 1, FF), jnp.float32, math.log(0.3), math.log(3.0)))
    ramp = jnp.arange(EXPERTS, dtype=jnp.float32) / max(EXPERTS - 1, 1)
    expert_scale = 0.6 * jnp.exp(ramp * math.log(3.0))
    values = base * columns * expert_scale[:, None, None, None] * replica_scale[None, :, None, None]
    return jnp.clip(values, -23.0, 23.0).astype(jnp.bfloat16)


def block_levels(rng, shape, shards, least, high):
    level, own = 1.0, jax.random.fold_in(rng, 6)
    for position, shards_of in shards:
        draws = jnp.exp(jax.random.uniform(jax.random.fold_in(own, position), (shards_of,), jnp.float32, least / len(shards), high / len(shards)))
        level = level * jnp.repeat(draws, shape[position] // shards_of).reshape([-1 if axis == position else 1 for axis in range(len(shape))])
    return level


def scatter_about(stream_key, dims, scale, most, cuts=(), held_as=jnp.bfloat16):
    gain = block_levels(stream_key, dims, cuts, -0.22, 0.18) if cuts else 1.0
    drawn = jax.random.normal(stream_key, dims, jnp.float32) * scale * gain
    return jnp.minimum(jnp.maximum(drawn, -most), most).astype(held_as)


def setup_inputs(seed: int = 0) -> dict:
    streams_of = jax.random.split(jax.random.key(seed), 4)
    return {
        "grad": draw_grad(jax.random.fold_in(streams_of[3], 71), 0),
        "error": scatter_about(streams_of[1], (EXPERTS, REPLICAS, ROWS, FF), 0.5, 3.0, ((0, 8), (1, 32))),
        "q_init": scatter_about(streams_of[2], (EXPERTS, R, FF), 1.0, 4.0, ((0, 8),)),
    }


def one_expert(pieces):
    grad_rows, error_rows, start_factor = pieces
    combined = (grad_rows.astype(jnp.float32) + error_rows.astype(jnp.float32)).astype(jnp.bfloat16)
    wide = combined.astype(jnp.float32)
    factor_low = start_factor
    orthonormal = jnp.zeros((ROWS, R), jnp.float32)
    ortho_low = orthonormal.astype(jnp.bfloat16)
    q_factor = jnp.zeros((R, FF), jnp.float32)
    for step in range(ITERS):
        projected = jnp.einsum('nrf,kf->rk', wide, factor_low.astype(jnp.float32), precision=lax.Precision.HIGHEST) / REPLICAS
        gram = jnp.dot(projected.T, projected, precision=lax.Precision.HIGHEST)
        lower_factor = jnp.linalg.cholesky(gram)
        orthonormal = jax.scipy.linalg.solve_triangular(lower_factor, projected.T, lower=True).T
        ortho_low = orthonormal.astype(jnp.bfloat16)
        q_factor = jnp.einsum('nrf,rk->kf', wide, ortho_low.astype(jnp.float32), precision=lax.Precision.HIGHEST) / REPLICAS
        factor_low = q_factor.astype(jnp.bfloat16)
    approx = jnp.dot(ortho_low.astype(jnp.float32), factor_low.astype(jnp.float32), preferred_element_type=jnp.float32)
    new_error = (wide - approx[None]).astype(jnp.bfloat16)
    squares = jnp.sum(jnp.square(new_error.astype(jnp.float32)))
    return (orthonormal, q_factor, new_error, squares)

def reference(grad, error, q_init):
    basis_out, q_factor, new_error, squares = lax.map(one_expert, (grad, error, q_init))
    count = EXPERTS * REPLICAS * ROWS * FF
    error_norm = jnp.sqrt(jnp.sum(squares) / count)
    return (basis_out, q_factor, new_error, error_norm)
```

```python
import functools

import jax
import jax.numpy as jnp
import numpy as np
from jax import lax
from jax.experimental import pallas as pl
from jax.experimental.pallas import tpu as pltpu
from jax.sharding import Mesh
from jax.sharding import PartitionSpec as P

F32 = jnp.float32
BF16 = jnp.bfloat16
HIGHEST = lax.Precision.HIGHEST
CHIPS = ("x", "y")
ALL = ("x", "y", "core", "expert")
VMEM_LIMIT = 48 * 1024 * 1024

NN = (((1,), (0,)), ((), ()))
NT = (((1,), (1,)), ((), ()))
TN = (((0,), (0,)), ((), ()))


def call(body, name, flops, moved, **kw):
    return pl.pallas_call(
        body,
        name=name,
        compiler_params=pltpu.CompilerParams(vmem_limit_bytes=VMEM_LIMIT),
        cost_estimate=pl.CostEstimate(flops=flops, bytes_accessed=moved, transcendentals=0),
        **kw,
    )


def combine(grad, error, q_init, parity, name):
    rows, ff = grad.shape
    rank = q_init.shape[0]
    width = 256
    pairs = ff // (2 * width)
    per = 2
    parity = jnp.reshape(parity, (1,)).astype(jnp.int32)

    def body(par_ref, *refs):
        g, e, q = refs[:per], refs[per : 2 * per], refs[2 * per : 3 * per]
        c_ref, p_ref = refs[3 * per :]
        step = pl.program_id(0)
        part = jnp.zeros((rank, rows), F32)
        for i in range(per):
            c = (g[i][...].astype(F32) + e[i][...].astype(F32)).astype(BF16)
            c_ref[i] = c
            part += lax.dot_general(q[i][...], c, NT, preferred_element_type=F32)

        @pl.when(step == 0)
        def _():
            p_ref[...] = part

        @pl.when(step > 0)
        def _():
            p_ref[...] += part

    def block(height, i):
        return pl.BlockSpec((height, width), lambda s, par: (0, 2 * (s * per + i) + par[0]))

    return call(
        body,
        name,
        2 * rows * rank * ff // 2,
        6 * rows * ff // 2,
        grid_spec=pltpu.PrefetchScalarGridSpec(
            num_scalar_prefetch=1,
            grid=(pairs // per,),
            in_specs=[block(rows, i) for i in range(per)] * 2 + [block(rank, i) for i in range(per)],
            out_specs=[
                pl.BlockSpec((per, rows, width), lambda s, par: (s, 0, 0)),
                pl.BlockSpec((rank, rows), lambda s, par: (0, 0)),
            ],
        ),
        out_shape=(
            jax.ShapeDtypeStruct((pairs, rows, width), BF16),
            jax.ShapeDtypeStruct((rank, rows), F32),
        ),
    )(parity, *([grad] * per), *([error] * per), *([q_init] * per))


def lanes_of(x):
    x = x.reshape(x.shape[0] // 8, 8, x.shape[1])
    x = jnp.sum(x, axis=0)
    return x[:, :128] + x[:, 128:]


def pair_sum(mine, other):
    pairs, rows, width = mine.shape
    per = 4

    def body(a_ref, b_ref, s_ref, d_ref):
        step = pl.program_id(0)
        part = jnp.zeros((8, 128), F32)
        for i in range(per):
            a, b = a_ref[i].astype(F32), b_ref[i].astype(F32)
            s_ref[i] = (a + b).astype(BF16)
            d = a - b
            part += lanes_of(d * d)
        part = 0.5 * part

        @pl.when(step == 0)
        def _():
            d_ref[...] = part

        @pl.when(step > 0)
        def _():
            d_ref[...] += part

    spec = pl.BlockSpec((per, rows, width), lambda s: (s, 0, 0))
    return call(
        body,
        "pair_sum",
        6 * mine.size,
        6 * mine.size,
        grid=(pairs // per,),
        in_specs=[spec, spec],
        out_specs=[spec, pl.BlockSpec((8, 128), lambda s: (0, 0))],
        out_shape=(
            jax.ShapeDtypeStruct(mine.shape, BF16),
            jax.ShapeDtypeStruct((8, 128), F32),
        ),
    )(mine, other)


def eliminate(p):
    rank = p.shape[0]
    g = lax.dot_general(p, p, NT, precision=HIGHEST, preferred_element_type=F32)
    row = lax.broadcasted_iota(jnp.int32, (rank, 1), 0)
    pivots = jnp.zeros((rank, 1), F32)
    for k in range(rank):
        column = g[:, k : k + 1]
        pivot = g[k : k + 1, k : k + 1]
        pivots = jnp.where(row == k, pivot, pivots)
        if k < rank - 1:
            factor = jnp.where(row > k, column / pivot, 0.0)
            g, p = g - factor * g[k : k + 1, :], p - factor * p[k : k + 1, :]
    return p / jnp.sqrt(pivots)


def orthonormal_of(parts, replicas):
    chips, rank, rows = parts.shape

    def body(p_ref, o_ref):
        o_ref[...] = eliminate(jnp.sum(p_ref[...], axis=0) * (1.0 / replicas))

    return call(
        body,
        "orthonormal",
        2 * rank * rank * rows,
        4 * parts.size,
        out_shape=jax.ShapeDtypeStruct((rank, rows), F32),
    )(parts)


def first_right(sums, ortho_t, replicas):
    chips, rows, width = sums.shape
    rank = ortho_t.shape[0]
    per = 4

    def body(s_ref, o_ref, mean_ref, p_ref):
        step = pl.program_id(0)
        total = jnp.sum(s_ref[...].astype(F32), axis=0)

        @pl.when(step == 0)
        def _():
            mean_ref[...] = total

        @pl.when(step > 0)
        def _():
            mean_ref[...] += total

        @pl.when(step == chips // per - 1)
        def _():
            mean = mean_ref[...] * (1.0 / replicas)
            mean_ref[...] = mean
            ortho_low = o_ref[...].astype(BF16).astype(F32)
            q = lax.dot_general(ortho_low, mean, NN, precision=HIGHEST, preferred_element_type=F32)
            low = q.astype(BF16).astype(F32)
            p_ref[...] = lax.dot_general(low, mean, NT, precision=HIGHEST, preferred_element_type=F32)

    return call(
        body,
        "first_right",
        4 * rank * rows * width,
        2 * sums.size,
        grid=(chips // per,),
        in_specs=[
            pl.BlockSpec((per, rows, width), lambda s: (s, 0, 0)),
            pl.BlockSpec((rank, rows), lambda s: (0, 0)),
        ],
        out_specs=[
            pl.BlockSpec((rows, width), lambda s: (0, 0)),
            pl.BlockSpec((rank, rows), lambda s: (0, 0)),
        ],
        out_shape=(
            jax.ShapeDtypeStruct((rows, width), F32),
            jax.ShapeDtypeStruct((rank, rows), F32),
        ),
    )(sums, ortho_t)


def second_right(parts, mean):
    chips, rank, rows = parts.shape
    width = mean.shape[1]

    def body(p_ref, m_ref, o_ref, low_ref, q_ref, f_ref):
        ortho_t = eliminate(jnp.sum(p_ref[...], axis=0))
        o_ref[...] = ortho_t
        low_t = ortho_t.astype(BF16)
        low_ref[...] = low_t.astype(F32).T.astype(BF16)
        q = lax.dot_general(low_t.astype(F32), m_ref[...], NN, precision=HIGHEST, preferred_element_type=F32)
        q_ref[...] = q
        f_ref[...] = jnp.broadcast_to(q.astype(BF16)[None], f_ref.shape)

    return call(
        body,
        "second_right",
        4 * rank * rows * width,
        4 * parts.size,
        out_shape=(
            jax.ShapeDtypeStruct((rank, rows), F32),
            jax.ShapeDtypeStruct((rows, rank), BF16),
            jax.ShapeDtypeStruct((rank, width), F32),
            jax.ShapeDtypeStruct((chips, rank, width), BF16),
        ),
    )(parts, mean)


def squares(sums, low, q, halves, copies):
    chips, rows, width = sums.shape
    per = 4

    def body(s_ref, low_ref, q_ref, h_ref, out_ref, a_ref, acc_ref):
        step = pl.program_id(0)

        @pl.when(step == 0)
        def _():
            a_ref[...] = 2.0 * lax.dot_general(
                low_ref[...], q_ref[...].astype(BF16), NN, preferred_element_type=F32
            )
            acc_ref[...] = h_ref[...]

        part = jnp.zeros((8, 128), F32)
        for i in range(per):
            d = s_ref[i].astype(F32) - a_ref[...]
            part += lanes_of(d * d)
        acc_ref[...] += 0.5 * part

        @pl.when(step == chips // per - 1)
        def _():
            out_ref[...] = jnp.broadcast_to(jnp.sum(acc_ref[...], axis=0, keepdims=True), out_ref.shape)

    return call(
        body,
        "squares",
        4 * sums.size,
        2 * sums.size,
        grid=(chips // per,),
        in_specs=[
            pl.BlockSpec((per, rows, width), lambda s: (s, 0, 0)),
            pl.BlockSpec(low.shape, lambda s: (0, 0)),
            pl.BlockSpec(q.shape, lambda s: (0, 0)),
            pl.BlockSpec((8, 128), lambda s: (0, 0)),
        ],
        out_specs=pl.BlockSpec((copies, 128), lambda s: (0, 0)),
        out_shape=jax.ShapeDtypeStruct((copies, 128), F32),
        scratch_shapes=[pltpu.VMEM((rows, width), F32), pltpu.VMEM((8, 128), F32)],
    )(sums, low, q, halves)


def residual(mine, other, low, f_mine, f_other, core):
    pairs, rows, width = mine.shape
    rank = low.shape[1]
    core = jnp.reshape(core, (1,)).astype(jnp.int32)
    per = 1

    def body(core_ref, a_ref, b_ref, low_ref, fa_ref, fb_ref, out_ref):
        low_v = low_ref[...]
        new_a = (
            a_ref[0].astype(F32)
            - lax.dot_general(low_v, fa_ref[0], NN, preferred_element_type=F32)
        ).astype(BF16)
        new_b = (
            b_ref[0].astype(F32)
            - lax.dot_general(low_v, fb_ref[0], NN, preferred_element_type=F32)
        ).astype(BF16)

        @pl.when(core_ref[0] == 0)
        def _():
            out_ref[:, :width] = new_a
            out_ref[:, width:] = new_b

        @pl.when(core_ref[0] != 0)
        def _():
            out_ref[:, :width] = new_b
            out_ref[:, width:] = new_a

    big = pl.BlockSpec((per, rows, width), lambda s, c: (s, 0, 0))
    small = pl.BlockSpec((per, rank, width), lambda s, c: (s, 0, 0))
    return call(
        body,
        "residual",
        4 * rank * rows * width * pairs,
        8 * mine.size,
        grid_spec=pltpu.PrefetchScalarGridSpec(
            num_scalar_prefetch=1,
            grid=(pairs // per,),
            in_specs=[big, big, pl.BlockSpec(low.shape, lambda s, c: (0, 0)), small, small],
            out_specs=pl.BlockSpec((rows, 2 * per * width), lambda s, c: (0, s)),
        ),
        out_shape=jax.ShapeDtypeStruct((rows, 2 * pairs * width), BF16),
    )(core, mine, other, low, f_mine, f_other)


def swap(x):
    return lax.ppermute(x, "core", [(0, 1), (1, 0)])


def to_chips(x, chips):
    return lax.all_to_all(jnp.broadcast_to(x[None], (chips,) + x.shape), CHIPS, 0, 0)


def local(grad, error, q_init):
    grad, error, q_init = grad[0, 0], error[0, 0], q_init[0]
    rows, ff = grad.shape
    chips = lax.axis_size(CHIPS)
    replicas = 2 * chips
    devices = lax.axis_size(ALL)
    core = lax.axis_index("core")

    sent, p_sent = combine(grad, error, q_init, 1 - core, "combine_sent")
    came = swap(sent)
    mine, p_mine = combine(grad, error, q_init, core, "combine_mine")

    left = p_sent + p_mine
    left = to_chips(left + swap(left), chips)

    pair, halves = pair_sum(mine, came)
    sums = lax.all_to_all(pair, CHIPS, 0, 0)

    ortho_t = orthonormal_of(left, replicas)
    mean, left = first_right(sums, ortho_t, replicas)
    left = to_chips(left + swap(left), chips)
    ortho_t, low, q, f = second_right(left, mean)

    f_mine = lax.all_to_all(f, CHIPS, 0, 0)
    f_other = swap(f_mine)
    total = lax.all_to_all(squares(sums, low, q, halves, devices), ALL, 0, 0)
    new_error = residual(mine, sent, low, f_mine, f_other, core)
    error_norm = jnp.sqrt(jnp.sum(total) / (rows * ff * devices))
    return (ortho_t.T[None], q[None], new_error[None, None], error_norm)


def solution(mesh):
    x = y = int(round(np.sqrt(mesh.shape["dp"] // 2)))
    fine = Mesh(mesh.devices.reshape(x, y, 2, mesh.shape["expert"]), ALL)
    dp = ("x", "y", "core")
    placed = (P("expert", dp, None, None), P("expert", dp, None, None), P("expert", None, None))
    return jax.shard_map(
        local,
        mesh=fine,
        in_specs=placed,
        out_specs=(
            P("expert", None, None),
            P("expert", None, dp),
            P("expert", dp, None, None),
            P(),
        ),
        check_vma=False,
    )
```

```python
import jax
import jax.numpy as jnp
import numpy as np
from jax import lax
from jax.experimental import pallas as pl
from jax.experimental.pallas import tpu as pltpu
from jax.sharding import Mesh
from jax.sharding import PartitionSpec as P

F32 = jnp.float32
BF16 = jnp.bfloat16
HIGHEST = lax.Precision.HIGHEST
CHIPS = ("x", "y")
ALL = ("x", "y", "core", "expert")

NN = (((1,), (0,)), ((), ()))
NT = (((1,), (1,)), ((), ()))
TN = (((0,), (0,)), ((), ()))


def call(body, name, flops, moved, vmem=8, **kw):
    return pl.pallas_call(
        body,
        name=name,
        compiler_params=pltpu.CompilerParams(vmem_limit_bytes=vmem * 1024 * 1024),
        cost_estimate=pl.CostEstimate(flops=flops, bytes_accessed=moved, transcendentals=0),
        **kw,
    )


IN_VMEM = pl.BlockSpec(memory_space=pltpu.VMEM)
IN_SMEM = pl.BlockSpec(memory_space=pltpu.SMEM)
IN_HBM = pl.BlockSpec(memory_space=pltpu.HBM)


def combine(grad, error, core, first, rows, vmem):
    ff = grad.shape[1]
    width = 256
    pairs = ff // (2 * width)
    step = 32

    def body(core_ref, g_hbm, e_hbm, c_ref, s_ref, g_ref, e_ref, sems):
        core = core_ref[0]
        cuts = [pl.ds(r, step) for r in range(0, rows, step)]
        copies = []
        for i, cut in enumerate(cuts):
            there = pl.ds(first + i * step, step)
            copies.append(
                (
                    pltpu.make_async_copy(g_hbm.at[there], g_ref.at[cut], sems.at[0, i]),
                    pltpu.make_async_copy(e_hbm.at[there], e_ref.at[cut], sems.at[1, i]),
                )
            )
            for copy in copies[-1]:
                copy.start()
        for copy, cut in zip(copies, cuts):
            finish(copy)
            for i in range(pairs):
                for parity, ref in ((core, c_ref), (1 - core, s_ref)):
                    own = pl.ds(pl.multiple_of((2 * i + parity) * width, width), width)
                    ref[i, cut] = (g_ref[cut, own].astype(F32) + e_ref[cut, own].astype(F32)).astype(BF16)

    blocks = jax.ShapeDtypeStruct((pairs, rows, width), BF16)
    return call(
        body,
        f"combine_{first}",
        rows * ff,
        6 * rows * ff,
        vmem=vmem,
        in_specs=[IN_SMEM, IN_HBM, IN_HBM],
        out_specs=[IN_VMEM] * 2,
        out_shape=[blocks, blocks],
        scratch_shapes=[
            pltpu.VMEM((rows, ff), BF16),
            pltpu.VMEM((rows, ff), BF16),
            pltpu.SemaphoreType.DMA((2, rows // step)),
        ],
    )(core, grad, error)


def project(mine, sent, q_init, core):
    runs = len(mine)
    pairs, rows, width = mine[0].shape
    rank = q_init.shape[0]
    half = rank // 2

    def body(core_ref, q_ref, *refs):
        a_refs, b_refs, (keep_ref, send_ref, p_ref) = refs[:runs], refs[runs : 2 * runs], refs[2 * runs :]
        core = core_ref[0]
        for r in range(runs):
            part = jnp.zeros((rows, rank), F32)
            for i in range(pairs):
                for parity, ref in ((core, a_refs[r]), (1 - core, b_refs[r])):
                    columns = pl.ds(pl.multiple_of((2 * i + parity) * width, width), width)
                    part += lax.dot_general(ref[i], q_ref[:, columns], NT, preferred_element_type=F32)
            p_ref[:, r * rows : (r + 1) * rows] = part.T
        keep_ref[...] = p_ref[pl.ds(pl.multiple_of(core * half, half), half)]
        send_ref[...] = p_ref[pl.ds(pl.multiple_of((1 - core) * half, half), half)]

    return call(
        body,
        "project",
        2 * rank * runs * rows * q_init.shape[1],
        4 * runs * mine[0].size,
        in_specs=[IN_SMEM] + [IN_VMEM] * (1 + 2 * runs),
        out_specs=[IN_VMEM] * 2,
        out_shape=[jax.ShapeDtypeStruct((half, runs * rows), F32)] * 2,
        scratch_shapes=[pltpu.VMEM((rank, runs * rows), F32)],
    )(core, q_init, *mine, *sent)


def finish(copies):
    for copy in copies:
        copy.wait()


def lanes_of(x):
    x = x.reshape(x.shape[0] // 8, 8, x.shape[1])
    x = jnp.sum(x, axis=0)
    return x[:, :128] + x[:, 128:]


def high_low(x):
    high = x.astype(BF16)
    return high, (x - high.astype(F32)).astype(BF16)


def pair_sum(mine, other, place, first, rest):
    pairs, rows, width = mine.shape
    side = int(round(np.sqrt(pairs)))
    full = 2 * rows
    half = 16
    height = side * full + 2 * half

    def body(place_ref, a_ref, b_ref, *refs):
        outs, d_ref = refs[-side - 1 : -1], refs[-1]
        core, own = place_ref[2], jnp.where(place_ref[2] == 0, place_ref[0], place_ref[1])
        total = jnp.zeros((8, 128), F32)
        for k in range(side):
            group = lax.rem(own + k, side)

            def step(j, total, k=k, group=group):
                i = jnp.where(core == 0, side * group + j, side * j + group)
                a, b = a_ref[i].astype(F32), b_ref[i].astype(F32)
                outs[k][pl.ds(pl.multiple_of(j * full + first, rows), rows)] = (a + b).astype(BF16)
                d = a - b
                return total + lanes_of(d * d)

            total = lax.fori_loop(0, side, step, total, unroll=True)
        total = 0.5 * total
        if rest:
            before_ref, p_ref, o_ref = refs[side : side + 3]
            d_ref[...] = total + before_ref[...]
            high, low = high_low(p_ref[...] + o_ref[...])
            for out in outs:
                out[side * full : side * full + half] = high
                out[side * full + half :] = low
        else:
            d_ref[...] = total

    return call(
        body,
        f"pair_sum_{first}",
        6 * mine.size,
        6 * mine.size,
        in_specs=[IN_SMEM] + [IN_VMEM] * (2 + len(rest)),
        out_specs=[IN_VMEM] * (side + 1),
        out_shape=[jax.ShapeDtypeStruct((height, width), BF16)] * side + [jax.ShapeDtypeStruct((8, 128), F32)],
        input_output_aliases={3 + k: k for k in range(side)} if rest else {},
    )(place, mine, other, *rest)


def two_terms(x):
    half = x.shape[0] // 2
    return x[:half].astype(F32) + x[half:].astype(F32)


def merge(parts, place, rows):
    side = len(parts)
    height, width = parts[0].shape
    more = height - side * rows

    def body(place_ref, *refs):
        ins, outs = refs[:side], refs[side:]
        own = jnp.where(place_ref[2] == 0, place_ref[1], place_ref[0])
        left = sum(two_terms(ref[side * rows :]) for ref in ins)
        high, low = high_low(left)
        for k in range(side):
            block = pl.multiple_of(lax.rem(own + k, side) * rows, rows)
            for r in range(0, rows, 64):
                part = pl.ds(block + r, 64)
                outs[k][r : r + 64] = sum(ref[part].astype(F32) for ref in ins).astype(BF16)
            outs[k][rows : rows + more // 2] = high
            outs[k][rows + more // 2 :] = low

    return call(
        body,
        "merge",
        side * height * width,
        4 * side * height * width,
        in_specs=[IN_SMEM] + [IN_VMEM] * side,
        out_specs=[IN_VMEM] * side,
        out_shape=[jax.ShapeDtypeStruct((rows + more, width), BF16)] * side,
    )(place, *parts)


def spread(parts, rows, weight, before):
    side = len(parts)

    def body(*refs):
        ins, before_ref, out_ref = refs[:side], refs[side], refs[side + 1]

        def step(r, total):
            part = pl.ds(pl.multiple_of(r * 64, 64), 64)
            values = [ref[part].astype(F32) for ref in ins]
            mean = sum(values) * (1.0 / side)
            for value in values:
                d = value - mean
                total += lanes_of(d * d)
            return total

        total = lax.fori_loop(0, rows // 64, step, jnp.zeros((8, 128), F32))
        out_ref[...] = before_ref[...] + weight * total

    return call(
        body,
        "spread",
        3 * side * rows * parts[0].shape[1],
        2 * side * rows * parts[0].shape[1],
        in_specs=[IN_VMEM] * (side + 1),
        out_specs=IN_VMEM,
        out_shape=jax.ShapeDtypeStruct((8, 128), F32),
    )(*parts, before)


def left_sum(parts, rows, after):
    side = len(parts)
    height, width = parts[0].shape

    def body(*refs):
        refs[-1][...] = sum(two_terms(ref[rows:]) for ref in refs[:side])

    return call(
        body,
        "left_sum",
        side * (height - rows) * width,
        2 * side * (height - rows) * width,
        in_specs=[IN_VMEM] * (side + 1),
        out_specs=IN_VMEM,
        out_shape=jax.ShapeDtypeStruct(((height - rows) // 2, width), F32),
    )(*parts, after)


def mean_of(parts, rows, replicas):
    side = len(parts)
    width = parts[0].shape[1]

    def body(*refs):
        refs[side][...] = sum(ref[:rows].astype(F32) for ref in refs[:side]) * (1.0 / replicas)

    return call(
        body,
        "mean",
        side * rows * width,
        2 * side * rows * width,
        in_specs=[IN_VMEM] * side,
        out_specs=IN_VMEM,
        out_shape=jax.ShapeDtypeStruct((rows, width), F32),
    )(*parts)


def eliminate(p):
    rank = p.shape[0]
    block = 4
    g = lax.dot_general(p, p, NT, precision=HIGHEST, preferred_element_type=F32)
    row = lax.broadcasted_iota(jnp.int32, (rank, 128), 0)
    pivots = jnp.ones((rank, 128), F32)
    for first in range(0, rank, block):
        columns = [jnp.broadcast_to(g[:, k : k + 1], (rank, 128)) for k in range(first, first + block)]
        for b in range(block):
            k = first + b
            pivot = columns[b][k : k + 1]
            pivots = jnp.where(row == k, pivot, pivots)
            factor = jnp.where(row > k, columns[b] / pivot, 0.0)
            for c in range(b + 1, block):
                columns[c] = columns[c] - factor * columns[c][k : k + 1]
            g = g - factor[:, :rank] * g[k : k + 1]
            p = jnp.concatenate(
                [p[:, l : l + 128] - factor * p[k : k + 1, l : l + 128] for l in range(0, p.shape[1], 128)], axis=1
            )
    scale = 1.0 / jnp.sqrt(pivots)
    return jnp.concatenate([p[:, l : l + 128] * scale for l in range(0, p.shape[1], 128)], axis=1)


def first_right(left, other_left, mean, core, replicas, after):
    half, rows = left.shape

    def body(core_ref, a_ref, b_ref, m_ref, after_ref, out_ref, p_ref):
        core = core_ref[0]
        p_ref[pl.ds(pl.multiple_of(core * half, half), half)] = a_ref[...]
        p_ref[pl.ds(pl.multiple_of((1 - core) * half, half), half)] = b_ref[...]
        ortho_low = eliminate(p_ref[...] * (1.0 / replicas)).astype(BF16).astype(F32)
        mean = m_ref[...]
        q = lax.dot_general(ortho_low, mean, NN, precision=HIGHEST, preferred_element_type=F32)
        low = q.astype(BF16).astype(F32)
        out_ref[...] = lax.dot_general(low, mean, NT, precision=HIGHEST, preferred_element_type=F32)

    return call(
        body,
        "first_right",
        8 * half * mean.size,
        4 * mean.size,
        in_specs=[IN_SMEM] + [IN_VMEM] * 4,
        out_specs=IN_VMEM,
        out_shape=jax.ShapeDtypeStruct((2 * half, rows), F32),
        scratch_shapes=[pltpu.VMEM((2 * half, rows), F32)],
    )(core, left, other_left, mean, after)


def add_copies(a, b, copies):
    def body(a_ref, b_ref, out_ref):
        out_ref[...] = jnp.broadcast_to((a_ref[...] + b_ref[...])[None], out_ref.shape)

    return call(
        body,
        "add_copies",
        a.size,
        4 * a.size * copies,
        in_specs=[IN_VMEM] * 2,
        out_specs=IN_VMEM,
        out_shape=jax.ShapeDtypeStruct((copies,) + a.shape, F32),
    )(a, b)


def second_right(parts, mean, spread_sum, replicas):
    chips, rank, rows = parts.shape
    width = mean.shape[1]
    more = 16

    def body(p_ref, m_ref, s_ref, o_ref, low_ref, q_ref, f_ref):
        total = p_ref[0]
        for i in range(1, chips):
            total += p_ref[i]
        ortho_t = eliminate(total)
        o_ref[...] = ortho_t
        low_t = ortho_t.astype(BF16)
        low = low_t.astype(F32).T.astype(BF16)
        low_ref[...] = low
        mean = m_ref[...]
        q = lax.dot_general(low_t.astype(F32), mean, NN, precision=HIGHEST, preferred_element_type=F32)
        q_ref[...] = q
        f = q.astype(BF16)
        d = mean - lax.dot_general(low, f, NN, preferred_element_type=F32)
        lanes = jnp.sum(s_ref[...] + replicas * lanes_of(d * d), axis=0, keepdims=True)
        high, rest = high_low(lanes)
        rest = lanes - high.astype(F32)
        middle, last = high_low(rest)
        row = lax.broadcasted_iota(jnp.int32, (more, 128), 0)
        terms = jnp.zeros((more, 128), F32)
        for i, term in enumerate((high, middle, last)):
            terms = jnp.where(row == i, term.astype(F32), terms)
        terms = jnp.concatenate([terms, jnp.zeros_like(terms)], axis=1).astype(BF16)
        f_ref[...] = jnp.broadcast_to(jnp.concatenate([f, terms], axis=0)[None], f_ref.shape)

    return call(
        body,
        "second_right",
        4 * rank * rows * width,
        4 * parts.size,
        in_specs=[IN_VMEM] * 3,
        out_specs=[IN_VMEM] * 4,
        out_shape=(
            jax.ShapeDtypeStruct((rank, rows), F32),
            jax.ShapeDtypeStruct((rows, rank), BF16),
            jax.ShapeDtypeStruct((rank, width), F32),
            jax.ShapeDtypeStruct((chips, rank + more, width), BF16),
        ),
    )(parts, mean, spread_sum)


def square_sum(f_mine, f_other, rank, copies):
    def body(a_ref, b_ref, out_ref):
        terms = a_ref[:, rank:].astype(F32) + b_ref[:, rank:].astype(F32)
        lanes = jnp.sum(jnp.sum(terms, axis=0), axis=0, keepdims=True)
        row = lax.broadcasted_iota(jnp.int32, (8, 128), 0)
        out_ref[...] = jnp.broadcast_to(jnp.where(row == 0, lanes[:, :128], 0.0)[None], out_ref.shape)

    return call(
        body,
        "square_sum",
        2 * f_mine.size,
        4 * f_mine.size,
        in_specs=[IN_VMEM] * 2,
        out_specs=IN_VMEM,
        out_shape=jax.ShapeDtypeStruct((copies, 8, 128), F32),
    )(f_mine, f_other)


def residual(mine, sent, low, f_mine, f_other, core):
    runs = len(mine)
    pairs, run, width = mine[0].shape
    rows, rank = low.shape
    ff = 2 * pairs * width

    def body(core_ref, low_ref, fa_ref, fb_ref, *refs):
        a_refs, b_refs, (out_hbm, out_ref, sems) = refs[:runs], refs[runs : 2 * runs], refs[2 * runs :]
        core = core_ref[0]
        low = low_ref[...]
        copies = []
        for i in range(pairs):
            for parity, c_refs, f_ref in ((core, a_refs, fa_ref), (1 - core, b_refs, fb_ref)):
                approx = lax.dot_general(low, f_ref[i, :rank], NN, preferred_element_type=F32)
                own = pl.ds(pl.multiple_of(parity * width, width), width)
                for r in range(runs):
                    cut = slice(r * run, (r + 1) * run)
                    out_ref[i, cut, own] = (c_refs[r][i].astype(F32) - approx[cut]).astype(BF16)
            columns = pl.ds(2 * i * width, 2 * width)
            copies.append(pltpu.make_async_copy(out_ref.at[i], out_hbm.at[:, columns], sems.at[i]))
            copies[-1].start()
        finish(copies)

    return call(
        body,
        "residual",
        2 * rank * rows * ff,
        4 * rows * ff,
        vmem=8,
        in_specs=[IN_SMEM] + [IN_VMEM] * (3 + 2 * runs),
        out_specs=IN_HBM,
        out_shape=jax.ShapeDtypeStruct((rows, ff), BF16),
        scratch_shapes=[pltpu.VMEM((pairs, rows, 2 * width), BF16), pltpu.SemaphoreType.DMA((pairs,))],
    )(core, low, f_mine, f_other, *mine, *sent)


def swap(x):
    return lax.ppermute(x, "core", [(0, 1), (1, 0)])


def shifted(parts, phase):
    side = len(parts)
    out = [parts[0]]
    for k in range(1, side):
        pairs = []
        for x in range(side):
            for y in range(side):
                for core in range(2):
                    to = ((x + k) % side, y) if core == phase else (x, (y + k) % side)
                    pairs.append(((x * side + y) * 2 + core, (to[0] * side + to[1]) * 2 + core))
        out.append(lax.ppermute(parts[k], ("x", "y", "core"), pairs))
    return out


def local(grad, error, q_init):
    grad, error, q_init = grad[0, 0], error[0, 0], q_init[0]
    rows, ff = grad.shape
    rank = q_init.shape[0]
    side, experts = lax.axis_size("x"), lax.axis_size("expert")
    chips = side * side
    replicas = 2 * chips
    place = jnp.stack([lax.axis_index(a) for a in ("x", "y", "core")]).astype(jnp.int32)
    core = jnp.reshape(lax.axis_index("core"), (1,)).astype(jnp.int32)

    run = rows // 2
    mine_a, sent_a = combine(grad, error, core, 0, run, 48)
    came_a = swap(sent_a)
    mine_b, sent_b = combine(grad, error, core, run, run, 46)
    came_b = swap(sent_b)
    left, left_sent = project([mine_a, mine_b], [sent_a, sent_b], q_init, core)
    before = pair_sum(mine_a, came_a, place, 0, ())
    *parts, squares = pair_sum(mine_b, came_b, place, run, (*before, left, swap(left_sent)))

    parts = shifted(parts, 0)
    before = spread(parts, side * rows, 0.5, squares)
    parts = shifted(merge(parts, place, rows), 1)
    squares = spread(parts, rows, 1.0 / (2 * side), before)

    left = left_sum(parts, rows, before)
    other_left = swap(left)
    mean = mean_of(parts, rows, replicas)
    left = first_right(left, other_left, mean, core, replicas, squares)
    parts = lax.all_to_all(add_copies(left, swap(left), chips), CHIPS, 0, 0)
    ortho_t, low, q, f = second_right(parts, mean, squares, replicas)

    f_mine = lax.all_to_all(f, CHIPS, 0, 0)
    f_other = swap(f_mine)
    total = lax.all_to_all(square_sum(f_mine, f_other, rank, experts), "expert", 0, 0)
    new_error = residual([mine_a, mine_b], [sent_a, sent_b], low, f_mine, f_other, core)
    error_norm = jnp.sqrt(jnp.sum(total) / (rows * ff * replicas * experts))
    return (ortho_t.T[None], q[None], new_error[None, None], error_norm)


def solution(mesh):
    x = y = int(round(np.sqrt(mesh.shape["dp"] // 2)))
    fine = Mesh(mesh.devices.reshape(x, y, 2, mesh.shape["expert"]), ALL)
    dp = ("x", "y", "core")
    placed = (P("expert", dp, None, None), P("expert", dp, None, None), P("expert", None, None))
    return jax.shard_map(
        local,
        mesh=fine,
        in_specs=placed,
        out_specs=(
            P("expert", None, None),
            P("expert", None, dp),
            P("expert", dp, None, None),
            P(),
        ),
        check_vma=False,
    )
```

```python
import jax
import jax.numpy as jnp
import numpy as np
from jax import lax
from jax.experimental import pallas as pl
from jax.experimental.pallas import tpu as pltpu
from jax.sharding import Mesh
from jax.sharding import PartitionSpec as P

F32 = jnp.float32
BF16 = jnp.bfloat16
HIGHEST = lax.Precision.HIGHEST
CHIPS = ("x", "y")
ALL = ("x", "y", "core", "expert")

NN = (((1,), (0,)), ((), ()))
NT = (((1,), (1,)), ((), ()))
TN = (((0,), (0,)), ((), ()))


def call(body, name, flops, moved, vmem=4, **kw):
    return pl.pallas_call(
        body,
        name=name,
        compiler_params=pltpu.CompilerParams(vmem_limit_bytes=vmem * 1024 * 1024),
        cost_estimate=pl.CostEstimate(flops=flops, bytes_accessed=moved, transcendentals=0),
        **kw,
    )


IN_VMEM = pl.BlockSpec(memory_space=pltpu.VMEM)
IN_SMEM = pl.BlockSpec(memory_space=pltpu.SMEM)
IN_HBM = pl.BlockSpec(memory_space=pltpu.HBM)


def combine(grad, error, core, first, rows, vmem, after=()):
    ff = grad.shape[1]
    width = 256
    pairs = ff // (2 * width)
    step = 32

    def body(core_ref, g_hbm, e_hbm, *refs):
        c_ref, s_ref, g_ref, e_ref, sems = refs[len(after) :]
        core = core_ref[0]
        cuts = [pl.ds(r, step) for r in range(0, rows, step)]
        copies = []
        for i, cut in enumerate(cuts):
            there = pl.ds(first + i * step, step)
            copies.append(
                (
                    pltpu.make_async_copy(g_hbm.at[there], g_ref.at[cut], sems.at[0, i]),
                    pltpu.make_async_copy(e_hbm.at[there], e_ref.at[cut], sems.at[1, i]),
                )
            )
            for copy in copies[-1]:
                copy.start()
        for copy, cut in zip(copies, cuts):
            finish(copy)
            for i in range(pairs):
                for parity, ref in ((core, c_ref), (1 - core, s_ref)):
                    own = pl.ds(pl.multiple_of((2 * i + parity) * width, width), width)
                    ref[i, cut] = (g_ref[cut, own].astype(F32) + e_ref[cut, own].astype(F32)).astype(BF16)

    blocks = jax.ShapeDtypeStruct((pairs, rows, width), BF16)
    return call(
        body,
        f"combine_{first}",
        rows * ff,
        6 * rows * ff,
        vmem=vmem,
        in_specs=[IN_SMEM, IN_HBM, IN_HBM] + [IN_VMEM] * len(after),
        out_specs=[IN_VMEM] * 2,
        out_shape=[blocks, blocks],
        scratch_shapes=[
            pltpu.VMEM((rows, ff), BF16),
            pltpu.VMEM((rows, ff), BF16),
            pltpu.SemaphoreType.DMA((2, rows // step)),
        ],
    )(core, grad, error, *after)


def project(mine, sent, q_init, core):
    runs = len(mine)
    pairs, rows, width = mine[0].shape
    rank = q_init.shape[0]
    half = rank // 2

    def body(core_ref, q_ref, *refs):
        a_refs, b_refs = refs[:runs], refs[runs : 2 * runs]
        keep_ref, send_ref, p_ref, s_ref, sem = refs[2 * runs :]
        core = core_ref[0]
        copy = pltpu.make_async_copy(b_refs[-1], s_ref, sem)
        copy.start()
        parts = [jnp.zeros((rows, rank), F32)] * runs
        for parity, c_refs in ((core, a_refs), (1 - core, [*b_refs[:-1], s_ref])):
            if c_refs[-1] is s_ref:
                copy.wait()
            for i in range(pairs):
                columns = pl.ds(pl.multiple_of((2 * i + parity) * width, width), width)
                for r in range(runs):
                    parts[r] += lax.dot_general(c_refs[r][i], q_ref[:, columns], NT, preferred_element_type=F32)
        p_ref[...] = jnp.concatenate([part.T for part in parts], axis=1)
        keep_ref[...] = p_ref[pl.ds(pl.multiple_of(core * half, half), half)]
        send_ref[...] = p_ref[pl.ds(pl.multiple_of((1 - core) * half, half), half)]

    return call(
        body,
        "project",
        2 * rank * runs * rows * q_init.shape[1],
        4 * runs * mine[0].size,
        in_specs=[IN_SMEM] + [IN_VMEM] * (2 * runs) + [IN_HBM],
        out_specs=[IN_VMEM] * 2,
        out_shape=[jax.ShapeDtypeStruct((half, runs * rows), F32)] * 2,
        scratch_shapes=[
            pltpu.VMEM((rank, runs * rows), F32),
            pltpu.VMEM((pairs, rows, width), BF16),
            pltpu.SemaphoreType.DMA,
        ],
    )(core, q_init, *mine, *sent)


def finish(copies):
    for copy in copies:
        copy.wait()


def lanes_of(x):
    x = x.reshape(x.shape[0] // 8, 8, x.shape[1])
    x = jnp.sum(x, axis=0)
    return x[:, :128] + x[:, 128:]


def high_low(x):
    high = x.astype(BF16)
    return high, (x - high.astype(F32)).astype(BF16)


def pair_sum(mine, other, place, left):
    runs = len(mine)
    pairs, rows, width = mine[0].shape
    side = int(round(np.sqrt(pairs)))
    half = left[0].shape[0]
    full = runs * rows
    height = side * full + 2 * half

    def body(place_ref, *refs):
        a_refs, b_refs, p_refs = refs[:runs], refs[runs : 2 * runs], refs[2 * runs : 2 * runs + 2]
        outs, t_ref, sems = refs[2 * runs + 2 : -2], refs[-2], refs[-1]
        core, own = place_ref[2], jnp.where(place_ref[2] == 0, place_ref[0], place_ref[1])
        copies = [pltpu.make_async_copy(b_refs[r], t_ref.at[r], sems.at[r]) for r in range(runs)]
        for copy in copies:
            copy.start()
        high, low = high_low(p_refs[0][...] + p_refs[1][...])
        for out in outs:
            out[side * full : side * full + half] = high
            out[side * full + half :] = low
        for r in range(runs):
            copies[r].wait()
            for k in range(side):
                group = lax.rem(own + k, side)
                for j in range(side):
                    i = jnp.where(core == 0, side * group + j, side * j + group)
                    there = j * full + r * rows
                    outs[k][there : there + rows] = a_refs[r][i] + t_ref[r, i]

    return call(
        body,
        "pair_sum",
        6 * runs * mine[0].size,
        6 * runs * mine[0].size,
        vmem=6,
        in_specs=[IN_SMEM] + [IN_VMEM] * runs + [IN_HBM] * runs + [IN_VMEM] * 2,
        out_specs=[IN_VMEM] * side,
        out_shape=[jax.ShapeDtypeStruct((height, width), BF16)] * side,
        scratch_shapes=[pltpu.VMEM((runs, pairs, rows, width), BF16), pltpu.SemaphoreType.DMA((runs,))],
    )(place, *mine, *other, *left)


def pair_spread(mine, other):
    runs = len(mine)
    pairs, rows, width = mine[0].shape

    def body(*refs):
        a_refs, b_refs, out_ref, t_ref, sems = refs[:runs], refs[runs : 2 * runs], refs[-3], refs[-2], refs[-1]
        copies = [pltpu.make_async_copy(b_refs[r], t_ref.at[r], sems.at[r]) for r in range(runs)]
        for copy in copies:
            copy.start()
        total = jnp.zeros((8, 128), F32)
        for r in range(runs):
            copies[r].wait()

            def step(i, total, r=r):
                d = a_refs[r][i].astype(F32) - t_ref[r, i].astype(F32)
                return total + lanes_of(d * d)

            total = lax.fori_loop(0, pairs, step, total)
        out_ref[...] = 0.5 * total

    return call(
        body,
        "pair_spread",
        3 * runs * mine[0].size,
        4 * runs * mine[0].size,
        vmem=6,
        in_specs=[IN_VMEM] * runs + [IN_HBM] * runs,
        out_specs=IN_VMEM,
        out_shape=jax.ShapeDtypeStruct((8, 128), F32),
        scratch_shapes=[pltpu.VMEM((runs, pairs, rows, width), BF16), pltpu.SemaphoreType.DMA((runs,))],
    )(*mine, *other)


def two_terms(x):
    half = x.shape[0] // 2
    return x[:half].astype(F32) + x[half:].astype(F32)


def merge(parts, place, rows, after):
    side = len(parts)
    height, width = parts[0].shape
    more = height - side * rows

    def body(place_ref, *refs):
        ins, outs = refs[:side], refs[side + 1 :]
        own = jnp.where(place_ref[2] == 0, place_ref[1], place_ref[0])
        if more:
            high, low = high_low(sum(two_terms(ref[side * rows :]) for ref in ins))
        for k in range(side):
            block = pl.multiple_of(lax.rem(own + k, side) * rows, rows)
            for r in range(0, rows, 64):
                part = pl.ds(block + r, 64)
                outs[k][r : r + 64] = sum(ref[part].astype(F32) for ref in ins).astype(BF16)
            if more:
                outs[k][rows : rows + more // 2] = high
                outs[k][rows + more // 2 :] = low

    return call(
        body,
        "merge_left" if more else "merge",
        side * height * width,
        4 * side * height * width,
        in_specs=[IN_SMEM] + [IN_VMEM] * (side + 1),
        out_specs=[IN_VMEM] * side,
        out_shape=[jax.ShapeDtypeStruct((rows + more, width), BF16)] * side,
    )(place, *parts, after)


def spread(parts, rows, weight, before):
    side, more = len(parts), len(before)

    def body(*refs):
        ins, befores, out_ref = refs[:side], refs[side : side + more], refs[-1]

        def step(r, total):
            part = pl.ds(pl.multiple_of(r * 64, 64), 64)
            values = [ref[part].astype(F32) for ref in ins]
            mean = sum(values) * (1.0 / side)
            for value in values:
                d = value - mean
                total += lanes_of(d * d)
            return total

        total = lax.fori_loop(0, rows // 64, step, jnp.zeros((8, 128), F32))
        out_ref[...] = sum(ref[...] for ref in befores) + weight * total

    return call(
        body,
        "spread",
        3 * side * rows * parts[0].shape[1],
        2 * side * rows * parts[0].shape[1],
        in_specs=[IN_VMEM] * (side + more),
        out_specs=IN_VMEM,
        out_shape=jax.ShapeDtypeStruct((8, 128), F32),
    )(*parts, *before)


def left_sum(parts, rows, after):
    side = len(parts)
    height, width = parts[0].shape

    def body(*refs):
        refs[-1][...] = sum(two_terms(ref[rows:]) for ref in refs[:side])

    return call(
        body,
        "left_sum",
        side * (height - rows) * width,
        2 * side * (height - rows) * width,
        in_specs=[IN_VMEM] * (side + 1),
        out_specs=IN_VMEM,
        out_shape=jax.ShapeDtypeStruct(((height - rows) // 2, width), F32),
    )(*parts, after)


def mean_of(runs, rows, replicas):
    side, width = len(runs[0]), runs[0][0].shape[1]

    def body(*refs):
        for r in range(len(runs)):
            ins = refs[r * side : (r + 1) * side]
            refs[-1][r * rows : (r + 1) * rows] = sum(ref[:rows].astype(F32) for ref in ins) * (1.0 / replicas)

    return call(
        body,
        "mean",
        len(runs) * side * rows * width,
        2 * len(runs) * side * rows * width,
        in_specs=[IN_VMEM] * (len(runs) * side),
        out_specs=IN_VMEM,
        out_shape=jax.ShapeDtypeStruct((len(runs) * rows, width), F32),
    )(*(part for parts in runs for part in parts))


def eliminate(p):
    rank = p.shape[0]
    block = 8
    g = lax.dot_general(p, p, NT, precision=HIGHEST, preferred_element_type=F32)
    row = lax.broadcasted_iota(jnp.int32, (rank, 128), 0)
    pivots = jnp.ones((rank, 128), F32)
    for first in range(0, rank, block):
        columns = [jnp.broadcast_to(g[:, k : k + 1], (rank, 128)) for k in range(first, first + block)]
        for b in range(block):
            k = first + b
            pivot = columns[b][k : k + 1]
            pivots = jnp.where(row == k, pivot, pivots)
            factor = jnp.where(row > k, columns[b] / pivot, 0.0)
            for c in range(b + 1, block):
                columns[c] = columns[c] - factor * columns[c][k : k + 1]
            g = g - factor[:, :rank] * g[k : k + 1]
            p = jnp.concatenate(
                [p[:, l : l + 128] - factor * p[k : k + 1, l : l + 128] for l in range(0, p.shape[1], 128)], axis=1
            )
    scale = 1.0 / jnp.sqrt(pivots)
    return jnp.concatenate([p[:, l : l + 128] * scale for l in range(0, p.shape[1], 128)], axis=1)


def first_right(left, other_left, mean, core, replicas, after):
    half, rows = left.shape

    def body(core_ref, a_ref, b_ref, m_ref, after_ref, out_ref, p_ref):
        core = core_ref[0]
        p_ref[pl.ds(pl.multiple_of(core * half, half), half)] = a_ref[...]
        p_ref[pl.ds(pl.multiple_of((1 - core) * half, half), half)] = b_ref[...]
        ortho_low = eliminate(p_ref[...] * (1.0 / replicas)).astype(BF16).astype(F32)
        mean = m_ref[...]
        q = lax.dot_general(ortho_low, mean, NN, precision=HIGHEST, preferred_element_type=F32)
        low = q.astype(BF16).astype(F32)
        out_ref[...] = lax.dot_general(low, mean, NT, precision=HIGHEST, preferred_element_type=F32)

    return call(
        body,
        "first_right",
        8 * half * mean.size,
        4 * mean.size,
        in_specs=[IN_SMEM] + [IN_VMEM] * 4,
        out_specs=IN_VMEM,
        out_shape=jax.ShapeDtypeStruct((2 * half, rows), F32),
        scratch_shapes=[pltpu.VMEM((2 * half, rows), F32)],
    )(core, left, other_left, mean, after)


def add_copies(a, b, copies):
    def body(a_ref, b_ref, out_ref):
        out_ref[...] = jnp.broadcast_to((a_ref[...] + b_ref[...])[None], out_ref.shape)

    return call(
        body,
        "add_copies",
        a.size,
        4 * a.size * copies,
        in_specs=[IN_VMEM] * 2,
        out_specs=IN_VMEM,
        out_shape=jax.ShapeDtypeStruct((copies,) + a.shape, F32),
    )(a, b)


def second_right(parts, mean, spread_sum, replicas):
    chips, rank, rows = parts.shape
    width = mean.shape[1]
    more = 16

    def body(p_ref, m_ref, s_ref, o_ref, low_ref, q_ref, f_ref):
        total = p_ref[0]
        for i in range(1, chips):
            total += p_ref[i]
        ortho_t = eliminate(total)
        o_ref[...] = ortho_t
        low_t = ortho_t.astype(BF16)
        low = low_t.astype(F32).T.astype(BF16)
        low_ref[...] = low_t
        mean = m_ref[...]
        q = lax.dot_general(low_t.astype(F32), mean, NN, precision=HIGHEST, preferred_element_type=F32)
        q_ref[...] = q
        f = q.astype(BF16)
        d = mean - lax.dot_general(low, f, NN, preferred_element_type=F32)
        lanes = jnp.sum(s_ref[...] + replicas * lanes_of(d * d), axis=0, keepdims=True)
        high, rest = high_low(lanes)
        rest = lanes - high.astype(F32)
        middle, last = high_low(rest)
        row = lax.broadcasted_iota(jnp.int32, (more, 128), 0)
        terms = jnp.zeros((more, 128), F32)
        for i, term in enumerate((high, middle, last)):
            terms = jnp.where(row == i, term.astype(F32), terms)
        terms = jnp.concatenate([terms, jnp.zeros_like(terms)], axis=1).astype(BF16)
        f_ref[...] = jnp.broadcast_to(jnp.concatenate([f, terms], axis=0)[None], f_ref.shape)

    return call(
        body,
        "second_right",
        4 * rank * rows * width,
        4 * parts.size,
        in_specs=[IN_VMEM] * 3,
        out_specs=[IN_VMEM] * 4,
        out_shape=(
            jax.ShapeDtypeStruct((rank, rows), F32),
            jax.ShapeDtypeStruct((rank, rows), BF16),
            jax.ShapeDtypeStruct((rank, width), F32),
            jax.ShapeDtypeStruct((chips, rank + more, width), BF16),
        ),
    )(parts, mean, spread_sum)


def square_sum(f_mine, f_other, rank, copies):
    chips, height, width = f_mine.shape
    more = height - rank

    def body(a_ref, b_hbm, out_hbm, b_ref, out_ref, sems):
        copy = pltpu.make_async_copy(b_hbm.at[:, pl.ds(rank, more)], b_ref, sems.at[0])
        copy.start()
        copy.wait()
        terms = a_ref[:, rank:].astype(F32) + b_ref[...].astype(F32)
        lanes = jnp.sum(jnp.sum(terms, axis=0), axis=0, keepdims=True)
        row = lax.broadcasted_iota(jnp.int32, (8, 128), 0)
        out_ref[...] = jnp.broadcast_to(jnp.where(row == 0, lanes[:, :128], 0.0)[None], out_ref.shape)
        copy = pltpu.make_async_copy(out_ref, out_hbm, sems.at[1])
        copy.start()
        copy.wait()

    return call(
        body,
        "square_sum",
        2 * f_mine.size,
        4 * f_mine.size,
        in_specs=[IN_VMEM, IN_HBM],
        out_specs=IN_HBM,
        out_shape=jax.ShapeDtypeStruct((copies, 8, 128), F32),
        scratch_shapes=[
            pltpu.VMEM((chips, more, width), BF16),
            pltpu.VMEM((copies, 8, 128), F32),
            pltpu.SemaphoreType.DMA((2,)),
        ],
    )(f_mine, f_other)


def root_mean(total, count):
    def body(t_ref, out_ref):
        out_ref[...] = jnp.sqrt(jnp.sum(t_ref[...], keepdims=True)[0] * (1.0 / count))

    return call(
        body,
        "root_mean",
        total.size,
        4 * total.size,
        in_specs=[IN_VMEM],
        out_specs=IN_VMEM,
        out_shape=jax.ShapeDtypeStruct((1, 1), F32),
    )(total)[0, 0]


def residual(mine, sent, low_t, f_mine, f_other, core):
    runs = len(mine)
    pairs, run, width = mine[0].shape
    rank, rows = low_t.shape
    ff = 2 * pairs * width

    def body(core_ref, low_ref, fa_ref, fb_ref, *refs):
        a_refs, b_refs = refs[:runs], list(refs[runs : 2 * runs])
        out_hbm, out_ref, s_ref, sems, s_sem = refs[2 * runs :]
        core = core_ref[0]
        arrive = pltpu.make_async_copy(b_refs[-1], s_ref, s_sem)
        arrive.start()
        b_refs[-1] = s_ref
        low = low_ref[...].astype(F32).T.astype(BF16)
        arrive.wait()
        copies = []
        for first in range(0, pairs, 4):
            for i in range(first, first + 4):
                for parity, c_refs, f_ref in ((core, a_refs, fa_ref), (1 - core, b_refs, fb_ref)):
                    approx = lax.dot_general(low, f_ref[i, :rank], NN, preferred_element_type=F32)
                    own = pl.ds(pl.multiple_of(parity * width, width), width)
                    for r in range(runs):
                        cut = slice(r * run, (r + 1) * run)
                        out_ref[i, cut, own] = (c_refs[r][i].astype(F32) - approx[cut]).astype(BF16)
            for i in range(first, first + 4):
                columns = pl.ds(2 * i * width, 2 * width)
                copies.append(pltpu.make_async_copy(out_ref.at[i], out_hbm.at[:, columns], sems.at[i]))
                copies[-1].start()
        finish(copies)

    return call(
        body,
        "residual",
        2 * rank * rows * ff,
        4 * rows * ff,
        vmem=8,
        in_specs=[IN_SMEM] + [IN_VMEM] * (2 + 2 * runs) + [IN_HBM],
        out_specs=IN_HBM,
        out_shape=jax.ShapeDtypeStruct((rows, ff), BF16),
        scratch_shapes=[
            pltpu.VMEM((pairs, rows, 2 * width), BF16),
            pltpu.VMEM((pairs, run, width), BF16),
            pltpu.SemaphoreType.DMA((pairs,)),
            pltpu.SemaphoreType.DMA,
        ],
    )(core, low_t, f_mine, f_other, *mine, *sent)


def swap(x):
    return lax.ppermute(x, "core", [(0, 1), (1, 0)])


def shifted(parts, phase):
    side = len(parts)
    out = [parts[0]]
    for k in range(1, side):
        pairs = []
        for x in range(side):
            for y in range(side):
                for core in range(2):
                    to = ((x + k) % side, y) if core == phase else (x, (y + k) % side)
                    pairs.append(((x * side + y) * 2 + core, (to[0] * side + to[1]) * 2 + core))
        out.append(lax.ppermute(parts[k], ("x", "y", "core"), pairs))
    return out


def local(grad, error, q_init):
    grad, error, q_init = grad[0, 0], error[0, 0], q_init[0]
    rows, ff = grad.shape
    rank = q_init.shape[0]
    side, experts = lax.axis_size("x"), lax.axis_size("expert")
    chips = side * side
    replicas = 2 * chips
    place = jnp.stack([lax.axis_index(a) for a in ("x", "y", "core")]).astype(jnp.int32)
    core = jnp.reshape(lax.axis_index("core"), (1,)).astype(jnp.int32)

    run = rows // 2
    mine_a, sent_a = combine(grad, error, core, 0, run, 48)
    came_a = swap(sent_a)
    mine_b, sent_b = combine(grad, error, core, run, run, 46, (mine_a,))
    came_b = swap(sent_b)
    left, left_sent = project([mine_a, mine_b], [sent_a, sent_b], q_init, core)
    parts = pair_sum([mine_a, mine_b], [came_a, came_b], place, (left, swap(left_sent)))

    parts = shifted(parts, 0)
    squares = pair_spread([mine_a, mine_b], [came_a, came_b])
    before = spread(parts, side * rows, 0.5, [squares])
    parts = shifted(merge(parts, place, rows, squares), 1)
    squares = spread(parts, rows, 1.0 / (2 * side), [before])

    left = left_sum(parts, rows, before)
    other_left = swap(left)
    mean = mean_of([parts], rows, replicas)
    left = first_right(left, other_left, mean, core, replicas, squares)
    parts = lax.all_to_all(add_copies(left, swap(left), chips), CHIPS, 0, 0)
    ortho_t, low, q, f = second_right(parts, mean, squares, replicas)

    f_mine = lax.all_to_all(f, CHIPS, 0, 0)
    f_other = swap(f_mine)
    total = lax.all_to_all(square_sum(f_mine, f_other, rank, experts), "expert", 0, 0)
    new_error = residual([mine_a, mine_b], [sent_a, sent_b], low, f_mine, f_other, core)
    error_norm = root_mean(total, rows * ff * replicas * experts)
    return (ortho_t.T[None], q[None], new_error[None, None], error_norm)


def solution(mesh):
    x = y = int(round(np.sqrt(mesh.shape["dp"] // 2)))
    fine = Mesh(mesh.devices.reshape(x, y, 2, mesh.shape["expert"]), ALL)
    dp = ("x", "y", "core")
    placed = (P("expert", dp, None, None), P("expert", dp, None, None), P("expert", None, None))
    return jax.shard_map(
        local,
        mesh=fine,
        in_specs=placed,
        out_specs=(
            P("expert", None, None),
            P("expert", None, dp),
            P("expert", dp, None, None),
            P(),
        ),
        check_vma=False,
    )
```

```python
import jax
import jax.numpy as jnp
import numpy as np
from jax import lax
from jax.experimental import pallas as pl
from jax.experimental.pallas import tpu as pltpu
from jax.sharding import Mesh
from jax.sharding import PartitionSpec as P

F32 = jnp.float32
BF16 = jnp.bfloat16
HIGHEST = lax.Precision.HIGHEST
CHIPS = ("x", "y")
ALL = ("x", "y", "core", "expert")

NN = (((1,), (0,)), ((), ()))
NT = (((1,), (1,)), ((), ()))
TN = (((0,), (0,)), ((), ()))


def call(body, name, flops, moved, vmem=4, **kw):
    return pl.pallas_call(
        body,
        name=name,
        compiler_params=pltpu.CompilerParams(vmem_limit_bytes=vmem * 1024 * 1024),
        cost_estimate=pl.CostEstimate(flops=flops, bytes_accessed=moved, transcendentals=0),
        **kw,
    )


IN_VMEM = pl.BlockSpec(memory_space=pltpu.VMEM)
IN_SMEM = pl.BlockSpec(memory_space=pltpu.SMEM)
IN_HBM = pl.BlockSpec(memory_space=pltpu.HBM)


def combine(grad, error, core, first, rows, vmem, after=()):
    ff = grad.shape[1]
    width = 256
    pairs = ff // (2 * width)
    step = 32

    def body(core_ref, g_hbm, e_hbm, *refs):
        c_ref, s_ref, g_ref, e_ref, sems = refs[len(after) :]
        core = core_ref[0]
        cuts = [pl.ds(r, step) for r in range(0, rows, step)]
        copies = []
        for i, cut in enumerate(cuts):
            there = pl.ds(first + i * step, step)
            copies.append(
                (
                    pltpu.make_async_copy(g_hbm.at[there], g_ref.at[cut], sems.at[0, i]),
                    pltpu.make_async_copy(e_hbm.at[there], e_ref.at[cut], sems.at[1, i]),
                )
            )
            for copy in copies[-1]:
                copy.start()
        for copy, cut in zip(copies, cuts):
            finish(copy)
            for i in range(pairs):
                for parity, ref in ((core, c_ref), (1 - core, s_ref)):
                    own = pl.ds(pl.multiple_of((2 * i + parity) * width, width), width)
                    ref[i, cut] = (g_ref[cut, own].astype(F32) + e_ref[cut, own].astype(F32)).astype(BF16)

    blocks = jax.ShapeDtypeStruct((pairs, rows, width), BF16)
    return call(
        body,
        f"combine_{first}",
        rows * ff,
        6 * rows * ff,
        vmem=vmem,
        in_specs=[IN_SMEM, IN_HBM, IN_HBM] + [IN_VMEM] * len(after),
        out_specs=[IN_VMEM] * 2,
        out_shape=[blocks, blocks],
        scratch_shapes=[
            pltpu.VMEM((rows, ff), BF16),
            pltpu.VMEM((rows, ff), BF16),
            pltpu.SemaphoreType.DMA((2, rows // step)),
        ],
    )(core, grad, error, *after)


def project(mine, sent, q_init, core):
    runs = len(mine)
    pairs, rows, width = mine[0].shape
    rank = q_init.shape[0]
    half = rank // 2

    def body(core_ref, q_ref, *refs):
        a_refs, b_refs = refs[:runs], refs[runs : 2 * runs]
        keep_ref, send_ref, p_ref, s_ref, sem = refs[2 * runs :]
        core = core_ref[0]
        copy = pltpu.make_async_copy(b_refs[-1], s_ref, sem)
        copy.start()
        parts = [jnp.zeros((rows, rank), F32)] * runs
        for parity, c_refs in ((core, a_refs), (1 - core, [*b_refs[:-1], s_ref])):
            if c_refs[-1] is s_ref:
                copy.wait()
            for i in range(pairs):
                columns = pl.ds(pl.multiple_of((2 * i + parity) * width, width), width)
                for r in range(runs):
                    parts[r] += lax.dot_general(c_refs[r][i], q_ref[:, columns], NT, preferred_element_type=F32)
        p_ref[...] = jnp.concatenate([part.T for part in parts], axis=1)
        keep_ref[...] = p_ref[pl.ds(pl.multiple_of(core * half, half), half)]
        send_ref[...] = p_ref[pl.ds(pl.multiple_of((1 - core) * half, half), half)]

    return call(
        body,
        "project",
        2 * rank * runs * rows * q_init.shape[1],
        4 * runs * mine[0].size,
        in_specs=[IN_SMEM] + [IN_VMEM] * (2 * runs) + [IN_HBM],
        out_specs=[IN_VMEM] * 2,
        out_shape=[jax.ShapeDtypeStruct((half, runs * rows), F32)] * 2,
        scratch_shapes=[
            pltpu.VMEM((rank, runs * rows), F32),
            pltpu.VMEM((pairs, rows, width), BF16),
            pltpu.SemaphoreType.DMA,
        ],
    )(core, q_init, *mine, *sent)


def finish(copies):
    for copy in copies:
        copy.wait()


def lanes_of(x):
    x = x.reshape(x.shape[0] // 8, 8, x.shape[1])
    x = jnp.sum(x, axis=0)
    return x[:, :128] + x[:, 128:]


def high_low(x):
    high = x.astype(BF16)
    return high, (x - high.astype(F32)).astype(BF16)


def pair_sum(mine, other, place, more):
    runs = len(mine)
    pairs, rows, width = mine[0].shape
    side = int(round(np.sqrt(pairs)))
    full = runs * rows
    height = side * full + more

    def body(place_ref, *refs):
        a_refs, b_refs = refs[:runs], refs[runs : 2 * runs]
        outs, t_ref, sems = refs[2 * runs : -2], refs[-2], refs[-1]
        core, own = place_ref[2], jnp.where(place_ref[2] == 0, place_ref[0], place_ref[1])
        copies = [pltpu.make_async_copy(b_refs[r], t_ref.at[r], sems.at[r]) for r in range(runs)]
        for copy in copies:
            copy.start()
        for out in outs:
            out[side * full :] = jnp.zeros((more, width), BF16)
        for r in range(runs):
            copies[r].wait()
            for k in range(side):
                group = lax.rem(own + k, side)
                for j in range(side):
                    i = jnp.where(core == 0, side * group + j, side * j + group)
                    there = j * full + r * rows
                    outs[k][there : there + rows] = a_refs[r][i] + t_ref[r, i]

    return call(
        body,
        "pair_sum",
        6 * runs * mine[0].size,
        6 * runs * mine[0].size,
        vmem=6,
        in_specs=[IN_SMEM] + [IN_VMEM] * runs + [IN_HBM] * runs,
        out_specs=[IN_VMEM] * side,
        out_shape=[jax.ShapeDtypeStruct((height, width), BF16)] * side,
        scratch_shapes=[pltpu.VMEM((runs, pairs, rows, width), BF16), pltpu.SemaphoreType.DMA((runs,))],
    )(place, *mine, *other)


def put_left(parts, a, b):
    side = len(parts)
    half = a.shape[0]
    height = parts[0].shape[0]

    def body(a_ref, b_ref, *refs):
        high, low = high_low(a_ref[...] + b_ref[...])
        for out in refs[side:]:
            out[height - 2 * half : height - half] = high
            out[height - half :] = low

    return call(
        body,
        "put_left",
        side * a.size,
        4 * side * a.size,
        in_specs=[IN_VMEM] * (2 + side),
        out_specs=[IN_VMEM] * side,
        out_shape=[jax.ShapeDtypeStruct(part.shape, BF16) for part in parts],
        input_output_aliases={2 + k: k for k in range(side)},
    )(a, b, *parts)


def pair_spread(mine, other):
    runs = len(mine)
    pairs, rows, width = mine[0].shape

    def body(*refs):
        a_refs, b_refs, out_ref, t_ref, sems = refs[:runs], refs[runs : 2 * runs], refs[-3], refs[-2], refs[-1]
        copies = [pltpu.make_async_copy(b_refs[r], t_ref.at[r], sems.at[r]) for r in range(runs)]
        for copy in copies:
            copy.start()
        total = jnp.zeros((8, 128), F32)
        for r in range(runs):
            copies[r].wait()

            def step(i, total, r=r):
                d = a_refs[r][i].astype(F32) - t_ref[r, i].astype(F32)
                return total + lanes_of(d * d)

            total = lax.fori_loop(0, pairs, step, total)
        out_ref[...] = 0.5 * total

    return call(
        body,
        "pair_spread",
        3 * runs * mine[0].size,
        4 * runs * mine[0].size,
        vmem=6,
        in_specs=[IN_VMEM] * runs + [IN_HBM] * runs,
        out_specs=IN_VMEM,
        out_shape=jax.ShapeDtypeStruct((8, 128), F32),
        scratch_shapes=[pltpu.VMEM((runs, pairs, rows, width), BF16), pltpu.SemaphoreType.DMA((runs,))],
    )(*mine, *other)


def two_terms(x):
    half = x.shape[0] // 2
    return x[:half].astype(F32) + x[half:].astype(F32)


def merge(parts, place, rows, after):
    side = len(parts)
    height, width = parts[0].shape
    more = height - side * rows

    def body(place_ref, *refs):
        ins, outs = refs[:side], refs[side + 1 :]
        own = jnp.where(place_ref[2] == 0, place_ref[1], place_ref[0])
        if more:
            high, low = high_low(sum(two_terms(ref[side * rows :]) for ref in ins))
        for k in range(side):
            block = pl.multiple_of(lax.rem(own + k, side) * rows, rows)
            for r in range(0, rows, 64):
                part = pl.ds(block + r, 64)
                outs[k][r : r + 64] = sum(ref[part].astype(F32) for ref in ins).astype(BF16)
            if more:
                outs[k][rows : rows + more // 2] = high
                outs[k][rows + more // 2 :] = low

    return call(
        body,
        "merge_left" if more else "merge",
        side * height * width,
        4 * side * height * width,
        in_specs=[IN_SMEM] + [IN_VMEM] * (side + 1),
        out_specs=[IN_VMEM] * side,
        out_shape=[jax.ShapeDtypeStruct((rows + more, width), BF16)] * side,
    )(place, *parts, after)


def spread(parts, rows, weight, before):
    side, more = len(parts), len(before)

    def body(*refs):
        ins, befores, out_ref = refs[:side], refs[side : side + more], refs[-1]

        def step(r, total):
            part = pl.ds(pl.multiple_of(r * 64, 64), 64)
            values = [ref[part].astype(F32) for ref in ins]
            mean = sum(values) * (1.0 / side)
            for value in values:
                d = value - mean
                total += lanes_of(d * d)
            return total

        total = lax.fori_loop(0, rows // 64, step, jnp.zeros((8, 128), F32))
        out_ref[...] = sum(ref[...] for ref in befores) + weight * total

    return call(
        body,
        "spread",
        3 * side * rows * parts[0].shape[1],
        2 * side * rows * parts[0].shape[1],
        in_specs=[IN_VMEM] * (side + more),
        out_specs=IN_VMEM,
        out_shape=jax.ShapeDtypeStruct((8, 128), F32),
    )(*parts, *before)


def left_sum(parts, rows, after):
    side = len(parts)
    height, width = parts[0].shape

    def body(*refs):
        refs[-1][...] = sum(two_terms(ref[rows:]) for ref in refs[:side])

    return call(
        body,
        "left_sum",
        side * (height - rows) * width,
        2 * side * (height - rows) * width,
        in_specs=[IN_VMEM] * (side + 1),
        out_specs=IN_VMEM,
        out_shape=jax.ShapeDtypeStruct(((height - rows) // 2, width), F32),
    )(*parts, after)


def mean_of(parts, rows, replicas):
    side, width = len(parts), parts[0].shape[1]

    def body(*refs):
        mean_ref, terms_ref, flipped_ref = refs[side:]
        mean = sum(ref[:rows].astype(F32) for ref in refs[:side]) * (1.0 / replicas)
        mean_ref[...] = mean
        high, low = high_low(mean)
        terms_ref[0] = high
        terms_ref[1] = low
        high, low = high_low(mean.T)
        flipped_ref[0] = high
        flipped_ref[1] = low

    return call(
        body,
        "mean",
        side * rows * width,
        2 * side * rows * width,
        in_specs=[IN_VMEM] * side,
        out_specs=[IN_VMEM] * 3,
        out_shape=(
            jax.ShapeDtypeStruct((rows, width), F32),
            jax.ShapeDtypeStruct((2, rows, width), BF16),
            jax.ShapeDtypeStruct((2, width, rows), BF16),
        ),
    )(*parts)


def product(x, terms_ref):
    return lax.dot_general(x, terms_ref[0], NN, preferred_element_type=F32) + lax.dot_general(
        x, terms_ref[1], NN, preferred_element_type=F32
    )


def eliminate(p):
    rank = p.shape[0]
    block = 8
    g = lax.dot_general(p, p, NT, precision=HIGHEST, preferred_element_type=F32)
    row = lax.broadcasted_iota(jnp.int32, (rank, 128), 0)
    pivots = jnp.ones((rank, 128), F32)
    for first in range(0, rank, block):
        columns = [jnp.broadcast_to(g[:, k : k + 1], (rank, 128)) for k in range(first, first + block)]
        for b in range(block):
            k = first + b
            pivot = columns[b][k : k + 1]
            pivots = jnp.where(row == k, pivot, pivots)
            factor = jnp.where(row > k, columns[b] / pivot, 0.0)
            for c in range(b + 1, block):
                columns[c] = columns[c] - factor * columns[c][k : k + 1]
            g = g - factor[:, :rank] * g[k : k + 1]
            p = jnp.concatenate(
                [p[:, l : l + 128] - factor * p[k : k + 1, l : l + 128] for l in range(0, p.shape[1], 128)], axis=1
            )
    scale = 1.0 / jnp.sqrt(pivots)
    return jnp.concatenate([p[:, l : l + 128] * scale for l in range(0, p.shape[1], 128)], axis=1)


def first_right(left, other_left, terms, flipped, core, replicas, after):
    half, rows = left.shape

    def body(core_ref, a_ref, b_ref, m_ref, t_ref, after_ref, out_ref, p_ref):
        core = core_ref[0]
        p_ref[pl.ds(pl.multiple_of(core * half, half), half)] = a_ref[...]
        p_ref[pl.ds(pl.multiple_of((1 - core) * half, half), half)] = b_ref[...]
        ortho_low = eliminate(p_ref[...] * (1.0 / replicas)).astype(BF16)
        out_ref[...] = product(product(ortho_low, m_ref).astype(BF16), t_ref)

    return call(
        body,
        "first_right",
        8 * half * terms.size,
        4 * terms.size,
        in_specs=[IN_SMEM] + [IN_VMEM] * 5,
        out_specs=IN_VMEM,
        out_shape=jax.ShapeDtypeStruct((2 * half, rows), F32),
        scratch_shapes=[pltpu.VMEM((2 * half, rows), F32)],
    )(core, left, other_left, terms, flipped, after)


def add_copies(a, b, copies):
    def body(a_ref, b_ref, out_ref):
        out_ref[...] = jnp.broadcast_to((a_ref[...] + b_ref[...])[None], out_ref.shape)

    return call(
        body,
        "add_copies",
        a.size,
        4 * a.size * copies,
        in_specs=[IN_VMEM] * 2,
        out_specs=IN_VMEM,
        out_shape=jax.ShapeDtypeStruct((copies,) + a.shape, F32),
    )(a, b)


def second_right(parts, mean, terms, spread_sum, replicas):
    chips, rank, rows = parts.shape
    width = mean.shape[1]
    more = 16

    def body(p_ref, m_ref, t_ref, s_ref, o_ref, low_ref, q_ref, f_ref):
        total = p_ref[0]
        for i in range(1, chips):
            total += p_ref[i]
        ortho_t = eliminate(total)
        o_ref[...] = ortho_t
        low_t = ortho_t.astype(BF16)
        low = low_t.astype(F32).T.astype(BF16)
        low_ref[...] = low_t
        mean = m_ref[...]
        q = product(low_t, t_ref)
        q_ref[...] = q
        f = q.astype(BF16)
        d = mean - lax.dot_general(low, f, NN, preferred_element_type=F32)
        lanes = jnp.sum(s_ref[...] + replicas * lanes_of(d * d), axis=0, keepdims=True)
        high, rest = high_low(lanes)
        rest = lanes - high.astype(F32)
        middle, last = high_low(rest)
        row = lax.broadcasted_iota(jnp.int32, (more, 128), 0)
        terms = jnp.zeros((more, 128), F32)
        for i, term in enumerate((high, middle, last)):
            terms = jnp.where(row == i, term.astype(F32), terms)
        terms = jnp.concatenate([terms, jnp.zeros_like(terms)], axis=1).astype(BF16)
        f_ref[...] = jnp.broadcast_to(jnp.concatenate([f, terms], axis=0)[None], f_ref.shape)

    return call(
        body,
        "second_right",
        4 * rank * rows * width,
        4 * parts.size,
        in_specs=[IN_VMEM] * 4,
        out_specs=[IN_VMEM] * 4,
        out_shape=(
            jax.ShapeDtypeStruct((rank, rows), F32),
            jax.ShapeDtypeStruct((rank, rows), BF16),
            jax.ShapeDtypeStruct((rank, width), F32),
            jax.ShapeDtypeStruct((chips, rank + more, width), BF16),
        ),
    )(parts, mean, terms, spread_sum)


def square_sum(f_mine, f_other, rank, copies):
    chips, height, width = f_mine.shape
    more = height - rank

    def body(a_ref, b_hbm, out_hbm, b_ref, out_ref, sems):
        copy = pltpu.make_async_copy(b_hbm.at[:, pl.ds(rank, more)], b_ref, sems.at[0])
        copy.start()
        copy.wait()
        terms = a_ref[:, rank:].astype(F32) + b_ref[...].astype(F32)
        lanes = jnp.sum(jnp.sum(terms, axis=0), axis=0, keepdims=True)
        row = lax.broadcasted_iota(jnp.int32, (8, 128), 0)
        out_ref[...] = jnp.broadcast_to(jnp.where(row == 0, lanes[:, :128], 0.0)[None], out_ref.shape)
        copy = pltpu.make_async_copy(out_ref, out_hbm, sems.at[1])
        copy.start()
        copy.wait()

    return call(
        body,
        "square_sum",
        2 * f_mine.size,
        4 * f_mine.size,
        in_specs=[IN_VMEM, IN_HBM],
        out_specs=IN_HBM,
        out_shape=jax.ShapeDtypeStruct((copies, 8, 128), F32),
        scratch_shapes=[
            pltpu.VMEM((chips, more, width), BF16),
            pltpu.VMEM((copies, 8, 128), F32),
            pltpu.SemaphoreType.DMA((2,)),
        ],
    )(f_mine, f_other)


def root_mean(total, count):
    def body(t_ref, out_ref):
        out_ref[...] = jnp.sqrt(jnp.sum(t_ref[...], keepdims=True)[0] * (1.0 / count))

    return call(
        body,
        "root_mean",
        total.size,
        4 * total.size,
        in_specs=[IN_VMEM],
        out_specs=IN_VMEM,
        out_shape=jax.ShapeDtypeStruct((1, 1), F32),
    )(total)[0, 0]


def residual(mine, sent, low_t, f_mine, f_other, core):
    runs = len(mine)
    pairs, run, width = mine[0].shape
    rank, rows = low_t.shape
    ff = 2 * pairs * width

    def body(core_ref, low_ref, fa_ref, fb_ref, *refs):
        a_refs, b_refs = refs[:runs], list(refs[runs : 2 * runs])
        out_hbm, out_ref, s_ref, sems, s_sem = refs[2 * runs :]
        core = core_ref[0]
        arrive = pltpu.make_async_copy(b_refs[-1], s_ref, s_sem)
        arrive.start()
        b_refs[-1] = s_ref
        low = low_ref[...].astype(F32).T.astype(BF16)
        arrive.wait()
        copies = []
        for first in range(0, pairs, 4):
            for i in range(first, first + 4):
                for parity, c_refs, f_ref in ((core, a_refs, fa_ref), (1 - core, b_refs, fb_ref)):
                    approx = lax.dot_general(low, f_ref[i, :rank], NN, preferred_element_type=F32)
                    own = pl.ds(pl.multiple_of(parity * width, width), width)
                    for r in range(runs):
                        cut = slice(r * run, (r + 1) * run)
                        out_ref[i, cut, own] = (c_refs[r][i].astype(F32) - approx[cut]).astype(BF16)
            for i in range(first, first + 4):
                columns = pl.ds(2 * i * width, 2 * width)
                copies.append(pltpu.make_async_copy(out_ref.at[i], out_hbm.at[:, columns], sems.at[i]))
                copies[-1].start()
        finish(copies)

    return call(
        body,
        "residual",
        2 * rank * rows * ff,
        4 * rows * ff,
        vmem=8,
        in_specs=[IN_SMEM] + [IN_VMEM] * (2 + 2 * runs) + [IN_HBM],
        out_specs=IN_HBM,
        out_shape=jax.ShapeDtypeStruct((rows, ff), BF16),
        scratch_shapes=[
            pltpu.VMEM((pairs, rows, 2 * width), BF16),
            pltpu.VMEM((pairs, run, width), BF16),
            pltpu.SemaphoreType.DMA((pairs,)),
            pltpu.SemaphoreType.DMA,
        ],
    )(core, low_t, f_mine, f_other, *mine, *sent)


def swap(x):
    return lax.ppermute(x, "core", [(0, 1), (1, 0)])


def shifted(parts, phase):
    side = len(parts)
    out = [parts[0]]
    for k in range(1, side):
        pairs = []
        for x in range(side):
            for y in range(side):
                for core in range(2):
                    to = ((x + k) % side, y) if core == phase else (x, (y + k) % side)
                    pairs.append(((x * side + y) * 2 + core, (to[0] * side + to[1]) * 2 + core))
        out.append(lax.ppermute(parts[k], ("x", "y", "core"), pairs))
    return out


def local(grad, error, q_init):
    grad, error, q_init = grad[0, 0], error[0, 0], q_init[0]
    rows, ff = grad.shape
    rank = q_init.shape[0]
    side, experts = lax.axis_size("x"), lax.axis_size("expert")
    chips = side * side
    replicas = 2 * chips
    place = jnp.stack([lax.axis_index(a) for a in ("x", "y", "core")]).astype(jnp.int32)
    core = jnp.reshape(lax.axis_index("core"), (1,)).astype(jnp.int32)

    run = rows // 2
    mine_a, sent_a = combine(grad, error, core, 0, run, 48)
    came_a = swap(sent_a)
    mine_b, sent_b = combine(grad, error, core, run, run, 46, (mine_a,))
    came_b = swap(sent_b)
    left, left_sent = project([mine_a, mine_b], [sent_a, sent_b], q_init, core)
    came_left = swap(left_sent)
    parts = pair_sum([mine_a, mine_b], [came_a, came_b], place, rank)
    parts = shifted(put_left(parts, left, came_left), 0)
    squares = pair_spread([mine_a, mine_b], [came_a, came_b])
    before = spread(parts, side * rows, 0.5, [squares])
    parts = shifted(merge(parts, place, rows, squares), 1)
    squares = spread(parts, rows, 1.0 / (2 * side), [before])

    left = left_sum(parts, rows, before)
    other_left = swap(left)
    mean, terms, flipped = mean_of(parts, rows, replicas)
    left = first_right(left, other_left, terms, flipped, core, replicas, squares)
    parts = lax.all_to_all(add_copies(left, swap(left), chips), CHIPS, 0, 0)
    ortho_t, low, q, f = second_right(parts, mean, terms, squares, replicas)

    f_mine = lax.all_to_all(f, CHIPS, 0, 0)
    f_other = swap(f_mine)
    total = lax.all_to_all(square_sum(f_mine, f_other, rank, experts), "expert", 0, 0)
    new_error = residual([mine_a, mine_b], [sent_a, sent_b], low, f_mine, f_other, core)
    error_norm = root_mean(total, rows * ff * replicas * experts)
    return (ortho_t.T[None], q[None], new_error[None, None], error_norm)


def solution(mesh):
    x = y = int(round(np.sqrt(mesh.shape["dp"] // 2)))
    fine = Mesh(mesh.devices.reshape(x, y, 2, mesh.shape["expert"]), ALL)
    dp = ("x", "y", "core")
    placed = (P("expert", dp, None, None), P("expert", dp, None, None), P("expert", None, None))
    return jax.shard_map(
        local,
        mesh=fine,
        in_specs=placed,
        out_specs=(
            P("expert", None, None),
            P("expert", None, dp),
            P("expert", dp, None, None),
            P(),
        ),
        check_vma=False,
    )
```

```python
import jax
import jax.numpy as jnp
import numpy as np
from jax import lax
from jax.experimental import pallas as pl
from jax.experimental.pallas import tpu as pltpu
from jax.sharding import Mesh
from jax.sharding import PartitionSpec as P

F32 = jnp.float32
BF16 = jnp.bfloat16
HIGHEST = lax.Precision.HIGHEST
CHIPS = ("x", "y")
ALL = ("x", "y", "core", "expert")

NN = (((1,), (0,)), ((), ()))
NT = (((1,), (1,)), ((), ()))
TN = (((0,), (0,)), ((), ()))


def call(body, name, flops, moved, vmem=4, **kw):
    return pl.pallas_call(
        body,
        name=name,
        compiler_params=pltpu.CompilerParams(vmem_limit_bytes=vmem * 1024 * 1024),
        cost_estimate=pl.CostEstimate(flops=flops, bytes_accessed=moved, transcendentals=0),
        **kw,
    )


IN_VMEM = pl.BlockSpec(memory_space=pltpu.VMEM)
IN_SMEM = pl.BlockSpec(memory_space=pltpu.SMEM)
IN_HBM = pl.BlockSpec(memory_space=pltpu.HBM)


def combine(grad, error, core, first, rows, vmem, after=()):
    ff = grad.shape[1]
    width = 256
    pairs = ff // (2 * width)
    step = 32

    def body(core_ref, g_hbm, e_hbm, *refs):
        c_ref, s_ref, g_ref, e_ref, sems = refs[len(after) :]
        core = core_ref[0]
        cuts = [pl.ds(r, step) for r in range(0, rows, step)]
        copies = []
        for i, cut in enumerate(cuts):
            there = pl.ds(first + i * step, step)
            copies.append(
                (
                    pltpu.make_async_copy(g_hbm.at[there], g_ref.at[cut], sems.at[0, i]),
                    pltpu.make_async_copy(e_hbm.at[there], e_ref.at[cut], sems.at[1, i]),
                )
            )
            for copy in copies[-1]:
                copy.start()
        for copy, cut in zip(copies, cuts):
            finish(copy)
            for i in range(pairs):
                for parity, ref in ((core, c_ref), (1 - core, s_ref)):
                    own = pl.ds(pl.multiple_of((2 * i + parity) * width, width), width)
                    ref[i, cut] = (g_ref[cut, own].astype(F32) + e_ref[cut, own].astype(F32)).astype(BF16)

    blocks = jax.ShapeDtypeStruct((pairs, rows, width), BF16)
    return call(
        body,
        f"combine_{first}",
        rows * ff,
        6 * rows * ff,
        vmem=vmem,
        in_specs=[IN_SMEM, IN_HBM, IN_HBM] + [IN_VMEM] * len(after),
        out_specs=[IN_VMEM] * 2,
        out_shape=[blocks, blocks],
        scratch_shapes=[
            pltpu.VMEM((rows, ff), BF16),
            pltpu.VMEM((rows, ff), BF16),
            pltpu.SemaphoreType.DMA((2, rows // step)),
        ],
    )(core, grad, error, *after)


def project(mine, sent, q_init, core):
    runs = len(mine)
    pairs, rows, width = mine[0].shape
    rank = q_init.shape[0]
    half = rank // 2

    def body(core_ref, q_ref, *refs):
        a_refs, b_refs = refs[:runs], refs[runs : 2 * runs]
        keep_ref, send_ref, p_ref, s_ref, sem = refs[2 * runs :]
        core = core_ref[0]
        copy = pltpu.make_async_copy(b_refs[-1], s_ref, sem)
        copy.start()
        parts = [jnp.zeros((rows, rank), F32)] * runs
        for parity, c_refs in ((core, a_refs), (1 - core, [*b_refs[:-1], s_ref])):
            if c_refs[-1] is s_ref:
                copy.wait()
            for i in range(pairs):
                columns = pl.ds(pl.multiple_of((2 * i + parity) * width, width), width)
                for r in range(runs):
                    parts[r] += lax.dot_general(c_refs[r][i], q_ref[:, columns], NT, preferred_element_type=F32)
        p_ref[...] = jnp.concatenate([part.T for part in parts], axis=1)
        keep_ref[...] = p_ref[pl.ds(pl.multiple_of(core * half, half), half)]
        send_ref[...] = p_ref[pl.ds(pl.multiple_of((1 - core) * half, half), half)]

    return call(
        body,
        "project",
        2 * rank * runs * rows * q_init.shape[1],
        4 * runs * mine[0].size,
        in_specs=[IN_SMEM] + [IN_VMEM] * (2 * runs) + [IN_HBM],
        out_specs=[IN_VMEM] * 2,
        out_shape=[jax.ShapeDtypeStruct((half, runs * rows), F32)] * 2,
        scratch_shapes=[
            pltpu.VMEM((rank, runs * rows), F32),
            pltpu.VMEM((pairs, rows, width), BF16),
            pltpu.SemaphoreType.DMA,
        ],
    )(core, q_init, *mine, *sent)


def finish(copies):
    for copy in copies:
        copy.wait()


def lanes_of(x):
    x = x.reshape(x.shape[0] // 8, 8, x.shape[1])
    x = jnp.sum(x, axis=0)
    return x[:, :128] + x[:, 128:]


def high_low(x):
    high = x.astype(BF16)
    return high, (x - high.astype(F32)).astype(BF16)


def pair_sum(mine, other, place, more):
    runs = len(mine)
    pairs, rows, width = mine[0].shape
    side = int(round(np.sqrt(pairs)))
    full = runs * rows
    height = side * full + more

    def body(place_ref, *refs):
        a_refs, b_refs = refs[:runs], refs[runs : 2 * runs]
        outs, t_ref, sems = refs[2 * runs : -2], refs[-2], refs[-1]
        core, own = place_ref[2], jnp.where(place_ref[2] == 0, place_ref[0], place_ref[1])
        copies = [pltpu.make_async_copy(b_refs[r], t_ref.at[r], sems.at[r]) for r in range(runs)]
        for copy in copies:
            copy.start()
        for out in outs:
            out[side * full :] = jnp.zeros((more, width), BF16)
        for r in range(runs):
            copies[r].wait()
            for k in range(side):
                group = lax.rem(own + k, side)
                for j in range(side):
                    i = jnp.where(core == 0, side * group + j, side * j + group)
                    there = j * full + r * rows
                    outs[k][there : there + rows] = a_refs[r][i] + t_ref[r, i]

    return call(
        body,
        "pair_sum",
        6 * runs * mine[0].size,
        6 * runs * mine[0].size,
        vmem=6,
        in_specs=[IN_SMEM] + [IN_VMEM] * runs + [IN_HBM] * runs,
        out_specs=[IN_VMEM] * side,
        out_shape=[jax.ShapeDtypeStruct((height, width), BF16)] * side,
        scratch_shapes=[pltpu.VMEM((runs, pairs, rows, width), BF16), pltpu.SemaphoreType.DMA((runs,))],
    )(place, *mine, *other)


def put_left(parts, a, b):
    side = len(parts)
    half = a.shape[0]
    height = parts[0].shape[0]

    def body(a_ref, b_ref, *refs):
        high, low = high_low(a_ref[...] + b_ref[...])
        for out in refs[side:]:
            out[height - 2 * half : height - half] = high
            out[height - half :] = low

    return call(
        body,
        "put_left",
        side * a.size,
        4 * side * a.size,
        in_specs=[IN_VMEM] * (2 + side),
        out_specs=[IN_VMEM] * side,
        out_shape=[jax.ShapeDtypeStruct(part.shape, BF16) for part in parts],
        input_output_aliases={2 + k: k for k in range(side)},
    )(a, b, *parts)


def pair_spread(mine, other):
    runs = len(mine)
    pairs, rows, width = mine[0].shape

    def body(*refs):
        a_refs, b_refs, out_ref, t_ref, sems = refs[:runs], refs[runs : 2 * runs], refs[-3], refs[-2], refs[-1]
        copies = [pltpu.make_async_copy(b_refs[r], t_ref.at[r], sems.at[r]) for r in range(runs)]
        for copy in copies:
            copy.start()
        total = jnp.zeros((8, 128), F32)
        for r in range(runs):
            copies[r].wait()

            def step(i, total, r=r):
                d = a_refs[r][i].astype(F32) - t_ref[r, i].astype(F32)
                return total + lanes_of(d * d)

            total = lax.fori_loop(0, pairs, step, total)
        out_ref[...] = 0.5 * total

    return call(
        body,
        "pair_spread",
        3 * runs * mine[0].size,
        4 * runs * mine[0].size,
        vmem=6,
        in_specs=[IN_VMEM] * runs + [IN_HBM] * runs,
        out_specs=IN_VMEM,
        out_shape=jax.ShapeDtypeStruct((8, 128), F32),
        scratch_shapes=[pltpu.VMEM((runs, pairs, rows, width), BF16), pltpu.SemaphoreType.DMA((runs,))],
    )(*mine, *other)


def two_terms(x):
    half = x.shape[0] // 2
    return x[:half].astype(F32) + x[half:].astype(F32)


def merge(parts, place, rows, after):
    side = len(parts)
    height, width = parts[0].shape
    more = height - side * rows

    def body(place_ref, *refs):
        ins, outs = refs[:side], refs[side + 1 :]
        own = jnp.where(place_ref[2] == 0, place_ref[1], place_ref[0])
        if more:
            high, low = high_low(sum(two_terms(ref[side * rows :]) for ref in ins))
        for k in range(side):
            block = pl.multiple_of(lax.rem(own + k, side) * rows, rows)
            for r in range(0, rows, 64):
                part = pl.ds(block + r, 64)
                outs[k][r : r + 64] = sum(ref[part].astype(F32) for ref in ins).astype(BF16)
            if more:
                outs[k][rows : rows + more // 2] = high
                outs[k][rows + more // 2 :] = low

    return call(
        body,
        "merge_left" if more else "merge",
        side * height * width,
        4 * side * height * width,
        in_specs=[IN_SMEM] + [IN_VMEM] * (side + 1),
        out_specs=[IN_VMEM] * side,
        out_shape=[jax.ShapeDtypeStruct((rows + more, width), BF16)] * side,
    )(place, *parts, after)


def spread(parts, rows, weight, before):
    side, more = len(parts), len(before)

    def body(*refs):
        ins, befores, out_ref = refs[:side], refs[side : side + more], refs[-1]

        def step(r, total):
            part = pl.ds(pl.multiple_of(r * 64, 64), 64)
            values = [ref[part].astype(F32) for ref in ins]
            mean = sum(values) * (1.0 / side)
            for value in values:
                d = value - mean
                total += lanes_of(d * d)
            return total

        total = lax.fori_loop(0, rows // 64, step, jnp.zeros((8, 128), F32))
        out_ref[...] = sum(ref[...] for ref in befores) + weight * total

    return call(
        body,
        "spread",
        3 * side * rows * parts[0].shape[1],
        2 * side * rows * parts[0].shape[1],
        in_specs=[IN_VMEM] * (side + more),
        out_specs=IN_VMEM,
        out_shape=jax.ShapeDtypeStruct((8, 128), F32),
    )(*parts, *before)


def left_sum(parts, rows, after):
    side = len(parts)
    height, width = parts[0].shape

    def body(*refs):
        refs[-1][...] = sum(two_terms(ref[rows:]) for ref in refs[:side])

    return call(
        body,
        "left_sum",
        side * (height - rows) * width,
        2 * side * (height - rows) * width,
        in_specs=[IN_VMEM] * (side + 1),
        out_specs=IN_VMEM,
        out_shape=jax.ShapeDtypeStruct(((height - rows) // 2, width), F32),
    )(*parts, after)


def mean_of(parts, rows, replicas):
    side, width = len(parts), parts[0].shape[1]

    def body(*refs):
        mean_ref, terms_ref, flipped_ref = refs[side:]
        mean = sum(ref[:rows].astype(F32) for ref in refs[:side]) * (1.0 / replicas)
        mean_ref[...] = mean
        high, low = high_low(mean)
        terms_ref[0] = high
        terms_ref[1] = low
        high, low = high_low(mean.T)
        flipped_ref[0] = high
        flipped_ref[1] = low

    return call(
        body,
        "mean",
        side * rows * width,
        2 * side * rows * width,
        in_specs=[IN_VMEM] * side,
        out_specs=[IN_VMEM] * 3,
        out_shape=(
            jax.ShapeDtypeStruct((rows, width), F32),
            jax.ShapeDtypeStruct((2, rows, width), BF16),
            jax.ShapeDtypeStruct((2, width, rows), BF16),
        ),
    )(*parts)


def product(x, terms_ref):
    return lax.dot_general(x, terms_ref[0], NN, preferred_element_type=F32) + lax.dot_general(
        x, terms_ref[1], NN, preferred_element_type=F32
    )


def eliminate(p):
    rank = p.shape[0]
    block = 8
    g = lax.dot_general(p, p, NT, precision=HIGHEST, preferred_element_type=F32)
    row = lax.broadcasted_iota(jnp.int32, (rank, 128), 0)
    pivots = jnp.ones((rank, 128), F32)
    for first in range(0, rank, block):
        columns = [jnp.broadcast_to(g[:, k : k + 1], (rank, 128)) for k in range(first, first + block)]
        for b in range(block):
            k = first + b
            pivot = columns[b][k : k + 1]
            pivots = jnp.where(row == k, pivot, pivots)
            factor = jnp.where(row > k, columns[b] / pivot, 0.0)
            for c in range(b + 1, block):
                columns[c] = columns[c] - factor * columns[c][k : k + 1]
            g = g - factor[:, :rank] * g[k : k + 1]
            p = jnp.concatenate(
                [p[:, l : l + 128] - factor * p[k : k + 1, l : l + 128] for l in range(0, p.shape[1], 128)], axis=1
            )
    scale = 1.0 / jnp.sqrt(pivots)
    return jnp.concatenate([p[:, l : l + 128] * scale for l in range(0, p.shape[1], 128)], axis=1)


def first_right(left, other_left, terms, flipped, core, replicas, after):
    half, rows = left.shape

    def body(core_ref, a_ref, b_ref, m_ref, t_ref, after_ref, keep_ref, send_ref, p_ref):
        core = core_ref[0]
        p_ref[pl.ds(pl.multiple_of(core * half, half), half)] = a_ref[...]
        p_ref[pl.ds(pl.multiple_of((1 - core) * half, half), half)] = b_ref[...]
        ortho_low = eliminate(p_ref[...] * (1.0 / replicas)).astype(BF16)
        p_ref[...] = product(product(ortho_low, m_ref).astype(BF16), t_ref)
        keep_ref[...] = p_ref[pl.ds(pl.multiple_of(core * half, half), half)]
        send_ref[...] = p_ref[pl.ds(pl.multiple_of((1 - core) * half, half), half)]

    return call(
        body,
        "first_right",
        8 * half * terms.size,
        4 * terms.size,
        in_specs=[IN_SMEM] + [IN_VMEM] * 5,
        out_specs=[IN_VMEM] * 2,
        out_shape=[jax.ShapeDtypeStruct((half, rows), F32)] * 2,
        scratch_shapes=[pltpu.VMEM((2 * half, rows), F32)],
    )(core, left, other_left, terms, flipped, after)


def add_copies(a, b, copies):
    def body(a_ref, b_ref, out_ref):
        out_ref[...] = jnp.broadcast_to((a_ref[...] + b_ref[...])[None], out_ref.shape)

    return call(
        body,
        "add_copies",
        a.size,
        4 * a.size * copies,
        in_specs=[IN_VMEM] * 2,
        out_specs=IN_VMEM,
        out_shape=jax.ShapeDtypeStruct((copies,) + a.shape, F32),
    )(a, b)


def chip_sum(parts):
    def body(p_ref, out_ref):
        total = p_ref[0]
        for i in range(1, parts.shape[0]):
            total += p_ref[i]
        out_ref[...] = total

    return call(
        body,
        "chip_sum",
        parts.size,
        4 * parts.size,
        in_specs=[IN_VMEM],
        out_specs=IN_VMEM,
        out_shape=jax.ShapeDtypeStruct(parts.shape[1:], F32),
    )(parts)


def second_right(left, other_left, mean, terms, spread_sum, core, chips, replicas):
    half, rows = left.shape
    rank = 2 * half
    width = mean.shape[1]
    more = 16

    def body(core_ref, a_ref, b_ref, m_ref, t_ref, s_ref, o_ref, low_ref, q_ref, f_ref, p_ref):
        core = core_ref[0]
        p_ref[pl.ds(pl.multiple_of(core * half, half), half)] = a_ref[...]
        p_ref[pl.ds(pl.multiple_of((1 - core) * half, half), half)] = b_ref[...]
        ortho_t = eliminate(p_ref[...])
        o_ref[...] = ortho_t
        low_t = ortho_t.astype(BF16)
        low = low_t.astype(F32).T.astype(BF16)
        low_ref[...] = low_t
        mean = m_ref[...]
        q = product(low_t, t_ref)
        q_ref[...] = q
        f = q.astype(BF16)
        d = mean - lax.dot_general(low, f, NN, preferred_element_type=F32)
        lanes = jnp.sum(s_ref[...] + replicas * lanes_of(d * d), axis=0, keepdims=True)
        high, rest = high_low(lanes)
        rest = lanes - high.astype(F32)
        middle, last = high_low(rest)
        row = lax.broadcasted_iota(jnp.int32, (more, 128), 0)
        terms = jnp.zeros((more, 128), F32)
        for i, term in enumerate((high, middle, last)):
            terms = jnp.where(row == i, term.astype(F32), terms)
        terms = jnp.concatenate([terms, jnp.zeros_like(terms)], axis=1).astype(BF16)
        f_ref[...] = jnp.broadcast_to(jnp.concatenate([f, terms], axis=0)[None], f_ref.shape)

    return call(
        body,
        "second_right",
        4 * rank * rows * width,
        4 * chips * rank * width,
        in_specs=[IN_SMEM] + [IN_VMEM] * 5,
        out_specs=[IN_VMEM] * 4,
        out_shape=(
            jax.ShapeDtypeStruct((rank, rows), F32),
            jax.ShapeDtypeStruct((rank, rows), BF16),
            jax.ShapeDtypeStruct((rank, width), F32),
            jax.ShapeDtypeStruct((chips, rank + more, width), BF16),
        ),
        scratch_shapes=[pltpu.VMEM((rank, rows), F32)],
    )(core, left, other_left, mean, terms, spread_sum)


def square_sum(f_mine, f_other, rank, copies):
    chips, height, width = f_mine.shape
    more = height - rank

    def body(a_ref, b_hbm, out_hbm, b_ref, out_ref, sems):
        copy = pltpu.make_async_copy(b_hbm.at[:, pl.ds(rank, more)], b_ref, sems.at[0])
        copy.start()
        copy.wait()
        terms = a_ref[:, rank:].astype(F32) + b_ref[...].astype(F32)
        lanes = jnp.sum(jnp.sum(terms, axis=0), axis=0, keepdims=True)
        row = lax.broadcasted_iota(jnp.int32, (8, 128), 0)
        out_ref[...] = jnp.broadcast_to(jnp.where(row == 0, lanes[:, :128], 0.0)[None], out_ref.shape)
        copy = pltpu.make_async_copy(out_ref, out_hbm, sems.at[1])
        copy.start()
        copy.wait()

    return call(
        body,
        "square_sum",
        2 * f_mine.size,
        4 * f_mine.size,
        in_specs=[IN_VMEM, IN_HBM],
        out_specs=IN_HBM,
        out_shape=jax.ShapeDtypeStruct((copies, 8, 128), F32),
        scratch_shapes=[
            pltpu.VMEM((chips, more, width), BF16),
            pltpu.VMEM((copies, 8, 128), F32),
            pltpu.SemaphoreType.DMA((2,)),
        ],
    )(f_mine, f_other)


def root_mean(total, count):
    def body(t_ref, out_ref):
        out_ref[...] = jnp.sqrt(jnp.sum(t_ref[...], keepdims=True)[0] * (1.0 / count))

    return call(
        body,
        "root_mean",
        total.size,
        4 * total.size,
        in_specs=[IN_VMEM],
        out_specs=IN_VMEM,
        out_shape=jax.ShapeDtypeStruct((1, 1), F32),
    )(total)[0, 0]


def residual(mine, sent, low_t, f_mine, f_other, core):
    runs = len(mine)
    pairs, run, width = mine[0].shape
    rank, rows = low_t.shape
    ff = 2 * pairs * width

    def body(core_ref, low_ref, fa_ref, fb_ref, *refs):
        a_refs, b_refs = refs[:runs], list(refs[runs : 2 * runs])
        out_hbm, out_ref, s_ref, sems, s_sem = refs[2 * runs :]
        core = core_ref[0]
        arrive = pltpu.make_async_copy(b_refs[-1], s_ref, s_sem)
        arrive.start()
        b_refs[-1] = s_ref
        low = low_ref[...].astype(F32).T.astype(BF16)
        arrive.wait()
        copies = []
        for first in range(0, pairs, 4):
            for i in range(first, first + 4):
                for parity, c_refs, f_ref in ((core, a_refs, fa_ref), (1 - core, b_refs, fb_ref)):
                    approx = lax.dot_general(low, f_ref[i, :rank], NN, preferred_element_type=F32)
                    own = pl.ds(pl.multiple_of(parity * width, width), width)
                    for r in range(runs):
                        cut = slice(r * run, (r + 1) * run)
                        out_ref[i, cut, own] = (c_refs[r][i].astype(F32) - approx[cut]).astype(BF16)
            for i in range(first, first + 4):
                columns = pl.ds(2 * i * width, 2 * width)
                copies.append(pltpu.make_async_copy(out_ref.at[i], out_hbm.at[:, columns], sems.at[i]))
                copies[-1].start()
        finish(copies)

    return call(
        body,
        "residual",
        2 * rank * rows * ff,
        4 * rows * ff,
        vmem=8,
        in_specs=[IN_SMEM] + [IN_VMEM] * (2 + 2 * runs) + [IN_HBM],
        out_specs=IN_HBM,
        out_shape=jax.ShapeDtypeStruct((rows, ff), BF16),
        scratch_shapes=[
            pltpu.VMEM((pairs, rows, 2 * width), BF16),
            pltpu.VMEM((pairs, run, width), BF16),
            pltpu.SemaphoreType.DMA((pairs,)),
            pltpu.SemaphoreType.DMA,
        ],
    )(core, low_t, f_mine, f_other, *mine, *sent)


def swap(x):
    return lax.ppermute(x, "core", [(0, 1), (1, 0)])


def shifted(parts, phase):
    side = len(parts)
    out = [parts[0]]
    for k in range(1, side):
        pairs = []
        for x in range(side):
            for y in range(side):
                for core in range(2):
                    to = ((x + k) % side, y) if core == phase else (x, (y + k) % side)
                    pairs.append(((x * side + y) * 2 + core, (to[0] * side + to[1]) * 2 + core))
        out.append(lax.ppermute(parts[k], ("x", "y", "core"), pairs))
    return out


def local(grad, error, q_init):
    grad, error, q_init = grad[0, 0], error[0, 0], q_init[0]
    rows, ff = grad.shape
    rank = q_init.shape[0]
    side, experts = lax.axis_size("x"), lax.axis_size("expert")
    chips = side * side
    replicas = 2 * chips
    place = jnp.stack([lax.axis_index(a) for a in ("x", "y", "core")]).astype(jnp.int32)
    core = jnp.reshape(lax.axis_index("core"), (1,)).astype(jnp.int32)

    run = rows // 2
    mine_a, sent_a = combine(grad, error, core, 0, run, 48)
    came_a = swap(sent_a)
    mine_b, sent_b = combine(grad, error, core, run, run, 46, (mine_a,))
    came_b = swap(sent_b)
    left, left_sent = project([mine_a, mine_b], [sent_a, sent_b], q_init, core)
    came_left = swap(left_sent)
    parts = pair_sum([mine_a, mine_b], [came_a, came_b], place, rank)
    parts = shifted(put_left(parts, left, came_left), 0)
    squares = pair_spread([mine_a, mine_b], [came_a, came_b])
    before = spread(parts, side * rows, 0.5, [squares])
    parts = shifted(merge(parts, place, rows, squares), 1)
    squares = spread(parts, rows, 1.0 / (2 * side), [before])

    left = left_sum(parts, rows, before)
    other_left = swap(left)
    mean, terms, flipped = mean_of(parts, rows, replicas)
    left, left_sent = first_right(left, other_left, terms, flipped, core, replicas, squares)
    left = chip_sum(lax.all_to_all(add_copies(left, swap(left_sent), chips), CHIPS, 0, 0))
    ortho_t, low, q, f = second_right(left, swap(left), mean, terms, squares, core, chips, replicas)

    f_mine = lax.all_to_all(f, CHIPS, 0, 0)
    f_other = swap(f_mine)
    total = lax.all_to_all(square_sum(f_mine, f_other, rank, experts), "expert", 0, 0)
    new_error = residual([mine_a, mine_b], [sent_a, sent_b], low, f_mine, f_other, core)
    error_norm = root_mean(total, rows * ff * replicas * experts)
    return (ortho_t.T[None], q[None], new_error[None, None], error_norm)


def solution(mesh):
    x = y = int(round(np.sqrt(mesh.shape["dp"] // 2)))
    fine = Mesh(mesh.devices.reshape(x, y, 2, mesh.shape["expert"]), ALL)
    dp = ("x", "y", "core")
    placed = (P("expert", dp, None, None), P("expert", dp, None, None), P("expert", None, None))
    return jax.shard_map(
        local,
        mesh=fine,
        in_specs=placed,
        out_specs=(
            P("expert", None, None),
            P("expert", None, dp),
            P("expert", dp, None, None),
            P(),
        ),
        check_vma=False,
    )
```
